32 devices in a mesh: lineage: 2 (over x), cells: 4 (over y, core), cols: 4 (over z).
Axes of the slice: x: 2, y: 2, z: 4, core: 2. Of those that a mesh axis runs over, the one named last changes fastest.
Arguments:
- positions: bfloat16 [128, 64, 512], P(('lineage', 'cells')), parts along dimension 0, may hold values from -1.5 to 1.5
- scales: bfloat16 [128, 512], P(('lineage', 'cells')), parts along dimension 0, may hold values from 1 to 2
- start_vectors: bfloat16 [128, 64, 512], P(('lineage', 'cells')), parts along dimension 0, may hold values from -6 to 6
- send_list: int32 [8, 4, 2], P(('lineage', 'cells')), parts along dimension 0, may hold values from 0 to 16, as said below
- pair_rows: int32 [8, 4, 48], P(('lineage', 'cells'), 'cols'), parts along dimension 0, may hold values from 0 to 15, as said below
- pair_partner: int32 [8, 4, 48], P(('lineage', 'cells'), 'cols'), parts along dimension 0, may hold values from 0 to 23, as said below
Outputs:
- subspace: float32 [128, 64, 512], P(('lineage', 'cells'), 'cols'), parts along dimension 0
The draws below stay inside these ranges and needn't reach their ends.
There are 2 independent parts, one for each index of `lineage`. The reference program is written for one: setup_inputs(seed, part) draws one part's arguments, and reference() takes and returns one part's arrays. A program takes and returns all parts, laid end to end along the dimension named above; each array names one. Nothing has to cross between parts.
Inputs may be any that keep to these rules, and one draw needn't show every extreme that they name: `send_list`: entries are local blocks of the sending group, distinct within one (sender, receiver) list and filling its first slots; 16 marks an empty slot; a group's slots for itself are empty; some group receives a full list from every other group and every group does from the group before it. `pair_rows`: every block of a cells group is paired with itself on some device of the group. `pair_partner`: A value of 16 or more always names a filled slot, and every filled slot a group receives is named by some pair of that group.
All inputs are finite; a program needn't handle non-finite values.
Results may differ from the reference program's by a relative error of at most 0.0047.
Values may be sent and summed in bfloat16 or wider, within the bound.
No kernel may reach another device: no remote copies, remote signals or barrier semaphores. Data moves between devices by JAX's collectives and lax.ppermute only.
A program may use at most 128 MiB of HBM per device.

```python
import math
import jax
import jax.numpy as jnp
from jax import lax

P_SIZE = 64
K = 64
BLOCK = 512
CAP = 2
ITERS = 2
BLK_DEV = 16
PAIRS_DEV = 48
NBLK = 64
N_CELLS = 4
N_COLS = 4


def pair_tables(key):
    keys = jax.random.split(key, 6)
    senders = jnp.arange(N_CELLS, dtype=jnp.int32)[:, None]
    takers = jnp.arange(N_CELLS, dtype=jnp.int32)[None, :]
    loads = jax.random.randint(keys[0], (N_CELLS, N_CELLS), 0, CAP + 1)
    busiest = jax.random.randint(keys[1], (), 0, N_CELLS)
    loads = jnp.where((takers == busiest) | (takers == (senders + 1) % N_CELLS), CAP, loads)
    loads = jnp.where(takers == senders, 0, loads)
    scores = jax.random.randint(keys[2], (N_CELLS, N_CELLS, BLK_DEV), 0, 1 << 20) * BLK_DEV + jnp.arange(BLK_DEV, dtype=jnp.int32)
    chosen = jnp.argsort(scores, axis=-1, stable=True)[:, :, :CAP].astype(jnp.int32)
    places = jnp.arange(CAP, dtype=jnp.int32)
    filled = places[None, None, :] < loads[:, :, None]
    send_table = jnp.where(filled, chosen, BLK_DEV).astype(jnp.int32)
    slot_total = N_CELLS * CAP
    received = jnp.transpose(filled, (1, 0, 2)).reshape(N_CELLS, slot_total).astype(jnp.int32)
    order = jnp.argsort(1 - received, axis=-1, stable=True).astype(jnp.int32)
    live = jnp.sum(received, axis=-1)
    firsts = (BLK_DEV + N_COLS - 1) // N_COLS
    others = PAIRS_DEV - firsts
    extra = N_COLS * others
    rank_scores = jax.random.randint(keys[3], (N_CELLS, extra), 0, 1 << 20) * extra + jnp.arange(extra, dtype=jnp.int32)
    ranks = jnp.argsort(jnp.argsort(rank_scores, axis=-1, stable=True), axis=-1, stable=True).astype(jnp.int32)
    picks = jax.random.randint(keys[4], (N_CELLS, extra), 0, BLK_DEV + live[:, None])
    picked_slot = jnp.take_along_axis(order, jnp.clip(picks - BLK_DEV, 0, slot_total - 1), axis=-1) + BLK_DEV
    random_partner = jnp.where(picks < BLK_DEV, picks, picked_slot)
    cover_slot = jnp.take_along_axis(order, jnp.clip(ranks, 0, slot_total - 1), axis=-1) + BLK_DEV
    partner_rest = jnp.where(ranks < live[:, None], cover_slot, random_partner)
    rows_rest = jax.random.randint(keys[5], (N_CELLS, extra), 0, BLK_DEV)
    column_ids = jnp.arange(N_COLS, dtype=jnp.int32)[:, None]
    steps_ids = jnp.arange(firsts, dtype=jnp.int32)[None, :]
    own_pairs = jnp.broadcast_to(((column_ids + N_COLS * steps_ids) % BLK_DEV)[None], (N_CELLS, N_COLS, firsts))
    row_table = jnp.concatenate([own_pairs, rows_rest.reshape(N_CELLS, N_COLS, others)], axis=-1).astype(jnp.int32)
    partner_table = jnp.concatenate([own_pairs, partner_rest.reshape(N_CELLS, N_COLS, others)], axis=-1).astype(jnp.int32)
    return (send_table, row_table, partner_table)


def draw_send_list(key, part):
    return pair_tables(key)[0]


def draw_pair_rows(key, part):
    return pair_tables(key)[1]


def draw_pair_partner(key, part):
    return pair_tables(key)[2]


def block_levels(stream_key, dims, cuts, least, top_value):
    factor_of, own = 1.0, jax.random.fold_in(stream_key, 6)
    for position, blocks in cuts:
        steps = jnp.exp(jax.random.uniform(jax.random.fold_in(own, position), (blocks,), jnp.float32, least / len(cuts), top_value / len(cuts)))
        factor_of = factor_of * jnp.repeat(steps, dims[position] // blocks).reshape([-1 if axis == position else 1 for axis in range(len(dims))])
    return factor_of


def gaussian(stream_key, shape, spread, reach, cuts=(), kind=jnp.bfloat16):
    entries = spread * jax.random.normal(stream_key, shape, jnp.float32)
    if cuts:
        entries = entries * block_levels(stream_key, shape, cuts, -0.22, 0.18)
    return jnp.clip(entries, -reach, reach).astype(kind)


def setup_inputs(seed: int = 0, part: int = 0) -> dict:
    seeds = jax.random.split(jax.random.key(seed), 7)
    own_keys = jax.random.split(jax.random.fold_in(seeds[6], part), 7)
    positions = gaussian(own_keys[0], (NBLK, P_SIZE, BLOCK), 0.25, 1.5, ((0, 4),))
    scales = jnp.clip(jnp.exp(math.log(2.0) - 0.6931472 * jax.random.uniform(own_keys[1], (NBLK, BLOCK), jnp.float32) ** block_levels(own_keys[1], (NBLK, BLOCK), ((0, 4),), -0.2, 0.2)), 1.0, 2.0).astype(jnp.bfloat16)
    start_vectors = gaussian(own_keys[2], (NBLK, K, BLOCK), 1.0, 6.0, ((0, 4),))
    send_list = draw_send_list(jax.random.fold_in(jax.random.fold_in(seeds[6], part), 71), part)
    pair_rows = draw_pair_rows(jax.random.fold_in(jax.random.fold_in(seeds[6], part), 71), part)
    pair_partner = draw_pair_partner(jax.random.fold_in(jax.random.fold_in(seeds[6], part), 71), part)
    return dict(positions=positions, scales=scales, start_vectors=start_vectors, send_list=send_list, pair_rows=pair_rows, pair_partner=pair_partner)


def kernel_tiles(points, spreads, square_norms, row_ids, partner_ids):
    left_points = jnp.take(points, row_ids, axis=0).astype(jnp.float32)
    right_points = jnp.take(points, partner_ids, axis=0).astype(jnp.float32)
    cross_terms = jnp.einsum('gpi,gpj->gij', left_points, right_points)
    distance = jnp.take(square_norms, row_ids, axis=0)[:, :, None] + jnp.take(square_norms, partner_ids, axis=0)[:, None, :] - 2.0 * cross_terms
    left_spread = jnp.take(spreads, row_ids, axis=0).astype(jnp.float32)
    right_spread = jnp.take(spreads, partner_ids, axis=0).astype(jnp.float32)
    kernel_width = left_spread[:, :, None] * right_spread[:, None, :]
    return jnp.exp(-distance / kernel_width).astype(jnp.bfloat16)

def global_pairs(send_list, pair_rows, pair_partner):
    owners = jnp.arange(N_CELLS, dtype=jnp.int32)[:, None, None]
    is_local = pair_partner < BLK_DEV
    slot_ids = jnp.maximum(pair_partner - BLK_DEV, 0)
    senders = (slot_ids // CAP).astype(jnp.int32)
    places = (slot_ids % CAP).astype(jnp.int32)
    takers = jnp.broadcast_to(owners, pair_partner.shape).astype(jnp.int32)
    remote = senders * BLK_DEV + send_list[senders, takers, places]
    partner_ids = jnp.where(is_local, owners * BLK_DEV + pair_partner, remote)
    row_ids = owners * BLK_DEV + pair_rows
    return (row_ids.reshape(-1).astype(jnp.int32), partner_ids.reshape(-1).astype(jnp.int32))

def reference(positions, scales, start_vectors, send_list, pair_rows, pair_partner):
    row_ids, partner_ids = global_pairs(send_list, pair_rows, pair_partner)
    bundle = 16
    rounds = row_ids.shape[0] // bundle
    row_groups = row_ids.reshape(rounds, bundle)
    partner_groups = partner_ids.reshape(rounds, bundle)
    mirrored = (partner_groups != row_groups).astype(jnp.float32)
    widened = positions.astype(jnp.float32)
    square_norms = lax.optimization_barrier(jnp.sum(widened * widened, axis=1))
    total_blocks = positions.shape[0]
    width_block = positions.shape[2]
    vector_count = start_vectors.shape[1]

    def make_tiles(group_index):
        return kernel_tiles(positions, scales, square_norms, row_groups[group_index], partner_groups[group_index])

    def degree_group(group_index, running):
        kernel = make_tiles(group_index).astype(jnp.float32)
        row_sums = lax.optimization_barrier(jnp.sum(kernel, axis=2))
        column_sums = lax.optimization_barrier(jnp.sum(kernel, axis=1)) * mirrored[group_index][:, None]
        running = running.at[row_groups[group_index]].add(row_sums)
        return running.at[partner_groups[group_index]].add(column_sums)
    degree = lax.fori_loop(0, rounds, degree_group, jnp.zeros((total_blocks, width_block), jnp.float32))
    inverse_root = lax.rsqrt(degree)
    subspace = start_vectors.astype(jnp.float32)
    for sweep_index in range(ITERS):
        scaled = (inverse_root[:, None, :] * subspace).astype(jnp.bfloat16)

        def vector_group(group_index, running):
            kernel = make_tiles(group_index).astype(jnp.float32)
            far_vectors = jnp.take(scaled, partner_groups[group_index], axis=0).astype(jnp.float32)
            row_vectors = jnp.take(scaled, row_groups[group_index], axis=0).astype(jnp.float32)
            forward = jnp.einsum('gkj,gij->gki', far_vectors, kernel)
            backward = jnp.einsum('gki,gij->gkj', row_vectors, kernel) * mirrored[group_index][:, None, None]
            running = running.at[row_groups[group_index]].add(forward)
            return running.at[partner_groups[group_index]].add(backward)
        summed = lax.fori_loop(0, rounds, vector_group, jnp.zeros((total_blocks, vector_count, width_block), jnp.float32))
        mapped = inverse_root[:, None, :] * summed
        gram_matrix = jnp.einsum('bkc,bjc->kj', mapped, mapped, precision=lax.Precision.HIGHEST) / (total_blocks * width_block)
        factor = jnp.linalg.cholesky(gram_matrix)
        inverse = lax.linalg.triangular_solve(factor, jnp.eye(vector_count, dtype=jnp.float32), left_side=True, lower=True)
        subspace = jnp.einsum('kj,bjc->bkc', inverse, mapped, precision=lax.Precision.HIGHEST)
    return subspace
```

```python
import math

import jax
import jax.numpy as jnp
from jax import lax
from jax.experimental import pallas as pl
from jax.experimental.pallas import tpu as pltpu
from jax.sharding import PartitionSpec as P

F32 = jnp.float32
BF16 = jnp.bfloat16
LOG2E = math.log2(math.e)
GROUP = 4
RING = 4
STORED = 160
DEPTH = 256
VMEM_BYTES = 56 * 2**20

VMEM_SPEC = pl.BlockSpec(memory_space=pltpu.VMEM)
SMEM_SPEC = pl.BlockSpec(memory_space=pltpu.SMEM)
ANY_SPEC = pl.BlockSpec(memory_space=pl.ANY)


def dot(a, b, ca, cb, precision=None):
    return lax.dot_general(
        a, b, (((ca,), (cb,)), ((), ())), preferred_element_type=F32, precision=precision
    )


def params():
    return pltpu.CompilerParams(vmem_limit_bytes=VMEM_BYTES)


def exchange(pieces, axis):
    n = lax.axis_size(axis)
    return [
        lax.ppermute(pieces[m], axis, [(i, i ^ m) for i in range(n)]) for m in range(1, n)
    ]


def spread(value, axis):
    n = lax.axis_size(axis)
    return [value] + [
        lax.ppermute(value, axis, [(i, (i + s) % n) for i in range(n)]) for s in range(1, n)
    ]


def butterfly(value, axis):
    n = lax.axis_size(axis)
    step = 1
    while step < n:
        value = value + lax.ppermute(value, axis, [(i, i ^ step) for i in range(n)])
        step *= 2
    return value


class Sizes:
    def __init__(self, positions, start, send_list, pair_rows):
        self.blocks, self.comps, self.width = positions.shape
        self.vectors = start.shape[1]
        self.peers = lax.axis_size("cells")
        self.cols = lax.axis_size("cols")
        self.cap = send_list.shape[2]
        self.slots = self.peers * self.cap
        self.own = self.blocks // self.cols
        self.pairs = pair_rows.shape[2] * self.cols
        self.long = 2 * self.pairs + GROUP
        self.short = self.pairs + GROUP
        self.r1, self.p1 = 0, self.long
        self.rs = 2 * self.long
        self.ps = self.rs + self.short
        self.r2 = self.ps + self.short
        self.p2 = self.r2 + self.short
        self.head = self.p2 + self.short
        self.mine = self.head + 8
        self.theirs = self.mine + self.slots
        self.table = self.theirs + self.slots


def build_table(sz, rows, partners, send_all, where):
    def kernel(rows_ref, partners_ref, send_ref, where_ref, tab):
        c = where_ref[0]
        z = where_ref[1]

        def lists(i, carry):
            m = i // sz.cap
            q = i % sz.cap
            tab[sz.mine + i] = send_ref[0, jnp.bitwise_xor(c, m) * sz.cap + q]
            tab[sz.theirs + i] = send_ref[m, c * sz.cap + q]
            return carry

        lax.fori_loop(0, sz.slots, lists, 0)

        def pair(i, carry):
            n1, ns, n2 = carry
            r = rows_ref[i]
            p = partners_ref[i]
            local = p < sz.blocks
            row_mine = (r // sz.own) == z
            slot = jnp.maximum(p - sz.blocks, 0)
            slot = jnp.bitwise_xor(slot // sz.cap, c) * sz.cap + slot % sz.cap
            slot_mine = (tab[sz.theirs + slot] // sz.own) == z
            base = z * sz.own
            tab[sz.r1 + n1] = r - base
            tab[sz.p1 + n1] = p
            n1 = n1 + jnp.where(jnp.logical_and(local, row_mine), 1, 0)
            tab[sz.r1 + n1] = p - base
            tab[sz.p1 + n1] = r
            both = jnp.logical_and(local, jnp.logical_and(p != r, (p // sz.own) == z))
            n1 = n1 + jnp.where(both, 1, 0)
            far = jnp.logical_not(local)
            tab[sz.r2 + n2] = r - base
            tab[sz.p2 + n2] = slot
            n2 = n2 + jnp.where(jnp.logical_and(far, row_mine), 1, 0)
            tab[sz.rs + ns] = slot
            tab[sz.ps + ns] = r
            ns = ns + jnp.where(jnp.logical_and(far, slot_mine), 1, 0)
            return n1, ns, n2

        zero = jnp.int32(0)
        n1, ns, n2 = lax.fori_loop(0, sz.pairs, pair, (zero, zero, zero))
        for i in range(GROUP):
            tab[sz.r1 + n1 + i] = sz.own
            tab[sz.p1 + n1 + i] = 0
            tab[sz.rs + ns + i] = sz.slots
            tab[sz.ps + ns + i] = 0
            tab[sz.r2 + n2 + i] = sz.own
            tab[sz.p2 + n2 + i] = 0
        tab[sz.head] = z
        tab[sz.head + 1] = (n1 + GROUP - 1) // GROUP
        tab[sz.head + 2] = (ns + GROUP - 1) // GROUP
        tab[sz.head + 3] = (n2 + GROUP - 1) // GROUP
        for i in range(4, 8):
            tab[sz.head + i] = 0

    return pl.pallas_call(
        kernel,
        out_shape=jax.ShapeDtypeStruct((sz.table,), jnp.int32),
        in_specs=[SMEM_SPEC] * 4,
        out_specs=SMEM_SPEC,
    )(rows, partners, send_all, where)


def split3(value):
    first = value.astype(BF16)
    rest = value - first.astype(F32)
    second = rest.astype(BF16)
    third = (rest - second.astype(F32)).astype(BF16)
    return first, second, third


def fill_factors(points, spread_row, left, right):
    comps = points.shape[0]
    x = points.astype(F32)
    inverse = 1.0 / spread_row
    norms = jnp.sum(x * x, axis=0, keepdims=True)
    y = x * (inverse * math.sqrt(2.0 * LOG2E))
    high = y.astype(BF16)
    low = (y - high.astype(F32)).astype(BF16)
    a1, a2, a3 = split3(norms * inverse * LOG2E)
    b1, b2, b3 = split3(inverse)
    left[0:comps] = high
    left[comps : 2 * comps] = low
    left[2 * comps : 3 * comps] = high
    right[0:comps] = high
    right[comps : 2 * comps] = high
    right[2 * comps : 3 * comps] = low
    rest = DEPTH - 3 * comps
    shape = (rest, points.shape[1])
    row = lax.broadcasted_iota(jnp.int32, shape, 0)
    lefts = (-a1, -a1, -a2, -a2, -a1, -a3, -b1, -b2, -b1, -b2, -b3, -b1)
    rights = (b1, b2, b1, b2, b3, b1, a1, a1, a2, a2, a1, a3)
    l_rest = jnp.zeros(shape, F32)
    r_rest = jnp.zeros(shape, F32)
    for k, (l_row, r_row) in enumerate(zip(lefts, rights)):
        l_rest = jnp.where(row == k, l_row.astype(F32), l_rest)
        r_rest = jnp.where(row == k, r_row.astype(F32), r_rest)
    left[3 * comps :] = l_rest.astype(BF16)
    right[3 * comps :] = r_rest.astype(BF16)


def segments(sz, tab, name):
    g1, gs, g2 = tab[sz.head + 1], tab[sz.head + 2], tab[sz.head + 3]
    if name == "1":
        return sz.r1, sz.p1, g1, 0
    if name == "S":
        return sz.rs, sz.ps, gs, g1
    return sz.r2, sz.p2, g2, g1 + gs


def row_block(sz, tab, name, row):
    if name == "S":
        return sz.blocks + jnp.minimum(row, sz.slots - 1)
    return tab[sz.head] * sz.own + jnp.minimum(row, sz.own - 1)


def partner_block(sz, name, partner):
    return sz.blocks + partner if name == "2" else partner


def build_tiles(sz, table, names, points, spreads, tiles, sums):
    first = tiles is None
    pieces = len(points)
    held = sz.blocks + (sz.slots if pieces > 1 else 0)
    sum_rows = sz.own + 1 + sz.slots + 1

    def kernel(*refs):
        tab = refs[0]
        point_refs = refs[1 : 1 + pieces]
        spread_refs = refs[1 + pieces : 1 + 2 * pieces]
        refs = refs[1 + 2 * pieces :]
        if not first:
            refs = refs[1:]
            old_sums, refs = refs[0], refs[1:]
        store, sum_ref, left, right, ring, sem = refs
        if first:
            sum_ref[...] = jnp.zeros(sum_ref.shape, F32)
        else:
            sum_ref[...] = old_sums[...]

        def local(b, carry):
            fill_factors(point_refs[0][b], spread_refs[0][b], left.at[b], right.at[b])
            return carry

        lax.fori_loop(0, sz.blocks, local, 0)
        for m in range(1, pieces):

            def far(q, carry, m=m):
                at = sz.blocks + m * sz.cap + q
                fill_factors(point_refs[m][q], spread_refs[m][q], left.at[at], right.at[at])
                return carry

            lax.fori_loop(0, sz.cap, far, 0)

        def write(slot, step):
            return pltpu.make_async_copy(
                ring.at[slot], store.at[pl.ds(step * GROUP, GROUP)], sem.at[slot]
            )

        done = jnp.int32(0)
        for name in names:
            rows, partners, steps, place = segments(sz, tab, name)
            base = 0 if name != "S" else sz.own + 1

            def step(t, carry, name=name, rows=rows, partners=partners, place=place, base=base, done=done):
                slot = lax.rem(done + t, 2)

                @pl.when(done + t >= 2)
                def _():
                    write(slot, 0).wait()

                for k in range(GROUP):
                    row = tab[rows + t * GROUP + k]
                    partner = tab[partners + t * GROUP + k]
                    r = row_block(sz, tab, name, row)
                    p = partner_block(sz, name, partner)
                    kernel_tile = jnp.exp2(dot(left[p], right[r], 0, 0))
                    ring[slot, k] = kernel_tile.astype(BF16)
                    sum_ref[base + row] += jnp.sum(
                        kernel_tile.reshape(sz.width // 8, 8, sz.width), axis=0
                    )
                write(slot, jnp.minimum(place + t, STORED // GROUP)).start()
                return carry

            lax.fori_loop(0, steps, step, 0)
            done = done + steps
        for slot in range(2):

            @pl.when(done >= slot + 1)
            def _(slot=slot):
                write(slot, 0).wait()

    tile_shape = jax.ShapeDtypeStruct((STORED + GROUP, sz.width, sz.width), BF16)
    sum_shape = jax.ShapeDtypeStruct((sum_rows, 8, sz.width), F32)
    args = [table] + points + spreads
    specs = [SMEM_SPEC] + [VMEM_SPEC] * (2 * pieces)
    aliases = {}
    if not first:
        aliases = {len(args): 0}
        args += [tiles, sums]
        specs += [ANY_SPEC, VMEM_SPEC]
    entries = 64 if first else 28
    return pl.pallas_call(
        kernel,
        out_shape=(tile_shape, sum_shape),
        in_specs=specs,
        out_specs=(ANY_SPEC, VMEM_SPEC),
        scratch_shapes=[
            pltpu.VMEM((held, DEPTH, sz.width), BF16),
            pltpu.VMEM((held, DEPTH, sz.width), BF16),
            pltpu.VMEM((2, GROUP, sz.width, sz.width), BF16),
            pltpu.SemaphoreType.DMA((2,)),
        ],
        input_output_aliases=aliases,
        compiler_params=params(),
        cost_estimate=pl.CostEstimate(
            flops=2 * entries * sz.width**2 * DEPTH,
            bytes_accessed=2 * entries * sz.width**2,
            transcendentals=entries * sz.width**2,
        ),
    )(*args)


def scale_start(sz, table, send_all, where, partial, start, start_far):
    def kernel(tab, send_ref, where_ref, *refs):
        parts = refs[: sz.peers]
        start_ref = refs[sz.peers]
        far_refs = refs[sz.peers + 1 : 2 * sz.peers]
        near_out, far_out, root_out, total = refs[2 * sz.peers :]
        c = where_ref[0]
        for m in range(sz.peers):
            total[m, 0 : sz.blocks] = parts[m][0 : sz.blocks]
        for m in range(sz.peers):
            for k in range(sz.peers):
                if k == m:
                    continue
                for q in range(sz.cap):
                    b = send_ref[m, jnp.bitwise_xor(c, k) * sz.cap + q]
                    at = sz.blocks + (k ^ m) * sz.cap + q
                    total[m, pl.ds(b, 1), :] += parts[k][at : at + 1, :]
        root = lax.rsqrt(total[0, 0 : sz.blocks])
        root_out[...] = root
        for b in range(sz.blocks):
            near_out[b] = (root[b : b + 1] * start_ref[b].astype(F32)).astype(BF16)
        far_out[0 : sz.cap] = jnp.zeros((sz.cap, sz.vectors, sz.width), BF16)
        for m in range(1, sz.peers):
            for q in range(sz.cap):
                b = jnp.minimum(tab[sz.theirs + m * sz.cap + q], sz.blocks - 1)
                far_root = lax.rsqrt(total[m, pl.ds(b, 1), :])
                far_out[m * sz.cap + q] = (far_root * far_refs[m - 1][q].astype(F32)).astype(BF16)

    return pl.pallas_call(
        kernel,
        out_shape=(
            jax.ShapeDtypeStruct((sz.blocks, sz.vectors, sz.width), BF16),
            jax.ShapeDtypeStruct((sz.slots, sz.vectors, sz.width), BF16),
            jax.ShapeDtypeStruct((sz.blocks, sz.width), F32),
        ),
        in_specs=[SMEM_SPEC] * 3 + [VMEM_SPEC] * (2 * sz.peers),
        out_specs=(VMEM_SPEC,) * 3,
        scratch_shapes=[pltpu.VMEM((sz.peers, sz.blocks + 8, sz.width), F32)],
        compiler_params=params(),
    )(table, send_all, where, *partial, start, *start_far)


def sweep_scratch(sz, held):
    return [
        pltpu.VMEM((held, sz.vectors, sz.width), BF16),
        pltpu.VMEM((RING, GROUP, sz.width, sz.width), BF16),
        pltpu.SemaphoreType.DMA((RING,)),
        pltpu.SemaphoreType.DMA((max(sz.cols, sz.peers),)),
        pltpu.VMEM((2, sz.comps, sz.width), BF16),
        pltpu.VMEM((2, 1, sz.width), F32),
        pltpu.VMEM((2, DEPTH, sz.width), BF16),
        pltpu.SemaphoreType.DMA((4,)),
    ]


class Stream:
    def __init__(self, sz, tab, name, store, geometry, scratch):
        self.sz, self.tab, self.name, self.store, self.geometry = sz, tab, name, store, geometry
        _, self.ring, self.sem, _, self.x, self.s, self.factors, self.xsem = scratch
        self.rows, self.partners, self.steps, self.place = segments(sz, tab, name)

    def read(self, t):
        slot = lax.rem(t, RING)
        return pltpu.make_async_copy(
            self.store.at[pl.ds((self.place + t) * GROUP, GROUP)], self.ring.at[slot], self.sem.at[slot]
        )

    def stored(self, t):
        return jnp.logical_and(t < self.steps, self.place + t < STORED // GROUP)

    def begin(self):
        for t in range(RING - 1):

            @pl.when(self.stored(t))
            def _(t=t):
                self.read(t).start()

    def rebuild(self, t):
        sz = self.sz
        slot = lax.rem(t, RING)

        def one(k, carry):
            row = self.tab[self.rows + t * GROUP + k]
            partner = self.tab[self.partners + t * GROUP + k]
            places = (
                partner_block(sz, self.name, partner),
                row_block(sz, self.tab, self.name, row),
            )
            for side, place in enumerate(places):
                copies = (
                    pltpu.make_async_copy(
                        self.geometry[0].at[place], self.x.at[side], self.xsem.at[2 * side]
                    ),
                    pltpu.make_async_copy(
                        self.geometry[1].at[place], self.s.at[side], self.xsem.at[2 * side + 1]
                    ),
                )
                for copy in copies:
                    copy.start()
                for copy in copies:
                    copy.wait()
            fill_factors(self.x[0], self.s[0], self.factors.at[0], self.factors.at[1])
            left = self.factors[0]
            fill_factors(self.x[1], self.s[1], self.factors.at[0], self.factors.at[1])
            self.ring[slot, k] = jnp.exp2(dot(left, self.factors[1], 0, 0)).astype(BF16)
            return carry

        lax.fori_loop(0, GROUP, one, 0)

    def run(self, vectors, offset, target):
        def step(t, carry):
            ahead = t + RING - 1

            @pl.when(self.stored(ahead))
            def _():
                self.read(ahead).start()

            have = self.stored(t)

            @pl.when(have)
            def _():
                self.read(t).wait()

            @pl.when(jnp.logical_not(have))
            def _():
                self.rebuild(t)

            slot = lax.rem(t, RING)
            for k in range(GROUP):
                row = self.tab[self.rows + t * GROUP + k]
                partner = self.tab[self.partners + t * GROUP + k] + offset
                target[row] += dot(vectors[partner], self.ring[slot, k], 1, 0)
            return carry

        lax.fori_loop(0, self.steps, step, 0)


def load_vectors(sz, tab, pieces, vbuf, sem):
    copies = []
    for s, piece in enumerate(pieces):
        if len(pieces) == 1:
            copies.append(pltpu.make_async_copy(piece, vbuf, sem.at[0]))
        else:
            owner = lax.rem(tab[sz.head] - s + sz.cols, sz.cols)
            copies.append(
                pltpu.make_async_copy(piece, vbuf.at[pl.ds(owner * sz.own, sz.own)], sem.at[s])
            )
    for copy in copies:
        copy.start()
    return copies


def sweep_cost(sz, entries):
    return pl.CostEstimate(
        flops=2 * entries * sz.width**2 * sz.vectors * 4,
        bytes_accessed=2 * entries * sz.width**2,
        transcendentals=0,
    )


def slot_products(sz, table, tiles, geometry, pieces, with_picks, kind):
    count = len(pieces)

    def kernel(tab, store, points, spreads, *refs):
        piece_refs, refs = refs[:count], refs[count:]
        out, refs = refs[0], refs[1:]
        if with_picks:
            picks, refs = refs[0], refs[1:]
        total, refs = refs[0], refs[1:]
        stream = Stream(sz, tab, "S", store, (points, spreads), refs)
        vbuf = refs[0]
        stream.begin()
        copies = load_vectors(sz, tab, piece_refs, vbuf, refs[3])
        total[...] = jnp.zeros(total.shape, F32)
        for copy in copies:
            copy.wait()
        if with_picks:
            for i in range(sz.slots):
                picks[i // sz.cap, i % sz.cap] = vbuf[jnp.minimum(tab[sz.mine + i], sz.blocks - 1)]
        stream.run(vbuf, 0, total)
        for i in range(sz.slots):
            out[i // sz.cap, i % sz.cap] = total[i].astype(kind)

    dims = (sz.peers, sz.cap, sz.vectors, sz.width)
    outs = (jax.ShapeDtypeStruct(dims, kind), jax.ShapeDtypeStruct(dims, BF16))
    outs = outs if with_picks else outs[:1]
    return pl.pallas_call(
        kernel,
        out_shape=outs,
        in_specs=[SMEM_SPEC] + [ANY_SPEC] * (3 + count),
        out_specs=(VMEM_SPEC,) * len(outs),
        scratch_shapes=[pltpu.VMEM((sz.slots + 1, sz.vectors, sz.width), F32)]
        + sweep_scratch(sz, sz.blocks),
        compiler_params=params(),
        cost_estimate=sweep_cost(sz, 12),
    )(table, tiles, *geometry, *pieces)


def local_products(sz, table, tiles, geometry, pieces):
    count = len(pieces)

    def kernel(tab, store, points, spreads, *refs):
        piece_refs, refs = refs[:count], refs[count:]
        out, total, refs = refs[0], refs[1], refs[2:]
        stream = Stream(sz, tab, "1", store, (points, spreads), refs)
        vbuf = refs[0]
        stream.begin()
        copies = load_vectors(sz, tab, piece_refs, vbuf, refs[3])
        total[...] = jnp.zeros(total.shape, F32)
        for copy in copies:
            copy.wait()
        stream.run(vbuf, 0, total)
        out[...] = total[0 : sz.own]

    return pl.pallas_call(
        kernel,
        out_shape=jax.ShapeDtypeStruct((sz.own, sz.vectors, sz.width), F32),
        in_specs=[SMEM_SPEC] + [ANY_SPEC] * (3 + count),
        out_specs=VMEM_SPEC,
        scratch_shapes=[pltpu.VMEM((sz.own + 1, sz.vectors, sz.width), F32)]
        + sweep_scratch(sz, sz.blocks),
        compiler_params=params(),
        cost_estimate=sweep_cost(sz, 64),
    )(table, tiles, *geometry, *pieces)


def far_products(sz, table, tiles, geometry, summed, far, returned, root, inverse):
    cells_total = sz.blocks * sz.width * sz.peers
    last = inverse is not None
    many = len(far)

    def kernel(tab, store, points, spreads, summed_ref, root_ref, *refs):
        if last:
            inverse_ref, refs = refs[0], refs[1:]
        far_refs, refs = refs[:many], refs[many:]
        back_refs, refs = refs[: sz.peers - 1], refs[sz.peers - 1 :]
        out, gram_out, total, refs = refs[0], refs[1], refs[2], refs[3:]
        stream = Stream(sz, tab, "2", store, (points, spreads), refs)
        vbuf, sem = refs[0], refs[3]
        stream.begin()
        if many == 1:
            copies = [pltpu.make_async_copy(far_refs[0], vbuf, sem.at[0])]
        else:
            copies = [
                pltpu.make_async_copy(far_refs[m - 1], vbuf.at[pl.ds(m * sz.cap, sz.cap)], sem.at[m])
                for m in range(1, sz.peers)
            ]
        for copy in copies:
            copy.start()
        z = tab[sz.head]
        total[0 : sz.own] = summed_ref[...]
        for m in range(1, sz.peers):
            for q in range(sz.cap):
                b = tab[sz.mine + m * sz.cap + q]
                place = jnp.where(b // sz.own == z, b - z * sz.own, sz.own)
                total[place] += back_refs[m - 1][q].astype(F32)
        for copy in copies:
            copy.wait()
        stream.run(vbuf, 0, total)
        gram = jnp.zeros((sz.vectors, sz.vectors), F32)
        for b in range(sz.own):
            root_row = root_ref[pl.ds(z * sz.own + b, 1), :]
            mapped = root_row * total[b]
            if last:
                mapped = dot(inverse_ref[...], mapped, 1, 0, lax.Precision.HIGHEST)
                out[b] = mapped
            else:
                out[b] = (root_row * mapped).astype(BF16)
            gram += dot(mapped, mapped, 1, 1, lax.Precision.HIGHEST)
        gram_out[...] = gram / cells_total

    args = [table, tiles, *geometry, summed, root]
    specs = [SMEM_SPEC] + [ANY_SPEC] * 3 + [VMEM_SPEC] * 2
    if last:
        args.append(inverse)
        specs.append(VMEM_SPEC)
    args += [*far, *returned]
    specs += [ANY_SPEC] * many + [VMEM_SPEC] * len(returned)
    return pl.pallas_call(
        kernel,
        out_shape=(
            jax.ShapeDtypeStruct((sz.own, sz.vectors, sz.width), F32 if last else BF16),
            jax.ShapeDtypeStruct((sz.vectors, sz.vectors), F32),
        ),
        in_specs=specs,
        out_specs=(VMEM_SPEC, VMEM_SPEC),
        scratch_shapes=[pltpu.VMEM((sz.own + 1, sz.vectors, sz.width), F32)]
        + sweep_scratch(sz, sz.slots),
        compiler_params=params(),
        cost_estimate=sweep_cost(sz, 20),
    )(*args)


def inverse_factor(gram):
    n = gram.shape[0]
    eye = (
        lax.broadcasted_iota(jnp.int32, (n, n), 0) == lax.broadcasted_iota(jnp.int32, (n, n), 1)
    ).astype(F32)
    whole = jnp.concatenate([gram, eye], axis=1)
    chunk = 8
    parts = [whole[i : i + chunk] for i in range(0, n, chunk)]
    row_ids = lax.broadcasted_iota(jnp.int32, (chunk, 1), 0)
    for k in range(n):
        at, inside = k // chunk, k % chunk
        row = parts[at][inside : inside + 1]
        pivot = row[:, k : k + 1]
        ratio = row / pivot
        for j in range(at, n // chunk):
            factor = parts[j][:, k : k + 1]
            if j == at:
                if inside == chunk - 1:
                    continue
                factor = jnp.where(row_ids > inside, factor, 0.0)
            parts[j] = parts[j] - factor * ratio
    out = []
    for j in range(n // chunk):
        diagonal = jnp.sum(
            parts[j][:, :n] * eye[j * chunk : (j + 1) * chunk], axis=1, keepdims=True
        )
        out.append(parts[j][:, n:] * lax.rsqrt(diagonal))
    return jnp.concatenate(out, axis=0)


def factor_call(sz, gram):
    def kernel(gram_ref, out):
        out[...] = inverse_factor(gram_ref[...])

    return pl.pallas_call(
        kernel,
        out_shape=jax.ShapeDtypeStruct((sz.vectors, sz.vectors), F32),
        in_specs=[VMEM_SPEC],
        out_specs=VMEM_SPEC,
    )(gram)


def normalize(sz, table, gram, mapped):
    share = sz.vectors // sz.cols

    def kernel(tab, gram_ref, mapped_ref, out, buf):
        inverse = inverse_factor(gram_ref[...])
        z = tab[sz.head]
        for b in range(sz.own):
            buf[...] = dot(inverse, mapped_ref[b], 1, 0, lax.Precision.HIGHEST)
            for s in range(sz.cols):
                to = lax.rem(z + s, sz.cols)
                out[s, b] = buf[pl.ds(pl.multiple_of(to * share, share), share)].astype(BF16)

    return pl.pallas_call(
        kernel,
        out_shape=jax.ShapeDtypeStruct((sz.cols, sz.own, share, sz.width), BF16),
        in_specs=[SMEM_SPEC, VMEM_SPEC, VMEM_SPEC],
        out_specs=VMEM_SPEC,
        scratch_shapes=[pltpu.VMEM((sz.vectors, sz.width), F32)],
        compiler_params=params(),
    )(table, gram, mapped)


def assemble(sz, table, pieces):
    share = sz.vectors // sz.cols

    def kernel(tab, *refs):
        out = refs[-1]
        z = tab[sz.head]
        for s in range(sz.cols):
            owner = lax.rem(z - s + sz.cols, sz.cols)
            for b in range(sz.own):
                out[owner * sz.own + b] = refs[s][b].astype(F32)

    return pl.pallas_call(
        kernel,
        out_shape=jax.ShapeDtypeStruct((sz.blocks, share, sz.width), F32),
        in_specs=[SMEM_SPEC] + [VMEM_SPEC] * sz.cols,
        out_specs=VMEM_SPEC,
        compiler_params=params(),
    )(table, *pieces)


def body(positions, scales, start_vectors, send_list, pair_rows, pair_partner):
    sz = Sizes(positions, start_vectors, send_list, pair_rows)
    c = lax.axis_index("cells")
    z = lax.axis_index("cols")
    where = jnp.stack([c, z]).astype(jnp.int32)

    pairs = jnp.concatenate([pair_rows.reshape(1, -1), pair_partner.reshape(1, -1)], axis=0)
    all_pairs = jnp.concatenate(spread(pairs, "cols"), axis=1)
    lists = send_list.reshape(1, -1)
    send_all = jnp.concatenate([lists] + exchange([lists] * sz.peers, "cells"), axis=0)

    relative = jnp.bitwise_xor(c, jnp.arange(sz.peers, dtype=jnp.int32))
    listed = jnp.take(send_list[0], relative, axis=0).reshape(-1)

    def pick(values):
        picked = jnp.take(values, listed, axis=0, mode="clip")
        return picked.reshape((sz.peers, sz.cap) + values.shape[1:])

    spreads = scales.astype(F32).reshape(sz.blocks, 1, sz.width)
    points_far = exchange(pick(positions), "cells")
    spreads_far = exchange(pick(spreads), "cells")
    start_far = exchange(pick(start_vectors), "cells")

    table = build_table(sz, all_pairs[0], all_pairs[1], send_all, where)
    tiles, sums = build_tiles(sz, table, ["1"], [positions], [spreads], None, None)
    tiles, sums = build_tiles(
        sz, table, ["S", "2"], [positions] + points_far, [spreads] + spreads_far, tiles, sums
    )
    geometry = (
        jnp.concatenate([positions, jnp.zeros_like(points_far[0])] + points_far, axis=0),
        jnp.concatenate([spreads, jnp.ones_like(spreads_far[0])] + spreads_far, axis=0),
    )

    column_sums = jnp.sum(sums, axis=1)
    owned = column_sums[: sz.own]
    slot_sums = column_sums[sz.own + 1 : sz.own + 1 + sz.slots]
    around = spread(jnp.concatenate([owned, slot_sums], axis=0), "cols")
    stacked = jnp.stack([piece[: sz.own] for piece in around])
    order = lax.rem(z - jnp.arange(sz.cols, dtype=jnp.int32) + sz.cols, sz.cols)
    group = jnp.take(stacked, order, axis=0).reshape(sz.blocks, sz.width)
    slot_total = sum(piece[sz.own :] for piece in around[1:]) + around[0][sz.own :]
    partial = jnp.concatenate([group, slot_total], axis=0)
    partials = [partial] + exchange([partial] * sz.peers, "cells")
    near, far, root = scale_start(sz, table, send_all, where, partials, start_vectors, start_far)

    (sent,) = slot_products(sz, table, tiles, geometry, [near], False, BF16)
    returned = exchange(sent, "cells")
    summed = local_products(sz, table, tiles, geometry, [near])
    scaled, gram = far_products(
        sz, table, tiles, geometry, summed, [far], returned, root, None
    )

    pieces = spread(scaled, "cols")
    gram = butterfly(butterfly(gram, "cells"), "cols")
    first_inverse = factor_call(sz, gram)
    sent, picks = slot_products(sz, table, tiles, geometry, pieces, True, F32)
    far_pieces = exchange(picks, "cells")
    returned = exchange(sent, "cells")
    summed = local_products(sz, table, tiles, geometry, pieces)
    mapped, gram = far_products(
        sz, table, tiles, geometry, summed, far_pieces, returned, root, first_inverse
    )
    gram = butterfly(butterfly(gram, "cells"), "cols")
    outgoing = normalize(sz, table, gram, mapped)
    n = sz.cols
    arrived = [outgoing[0]] + [
        lax.ppermute(outgoing[s], "cols", [(i, (i + s) % n) for i in range(n)]) for s in range(1, n)
    ]
    return assemble(sz, table, arrived)


def solution(mesh):
    in_specs = (
        P(("lineage", "cells"), None, None),
        P(("lineage", "cells"), None),
        P(("lineage", "cells"), None, None),
        P(("lineage", "cells"), None, None),
        P(("lineage", "cells"), "cols", None),
        P(("lineage", "cells"), "cols", None),
    )
    out_specs = P(("lineage", "cells"), "cols", None)
    return jax.shard_map(body, mesh=mesh, in_specs=in_specs, out_specs=out_specs, check_vma=False)
```

```python
import math

import jax
import jax.numpy as jnp
from jax import lax
from jax.experimental import pallas as pl
from jax.experimental.pallas import tpu as pltpu
from jax.sharding import PartitionSpec as P

F32 = jnp.float32
BF16 = jnp.bfloat16
LOG2E = math.log2(math.e)
GROUP = 4
RING = 4
STORED = 160
DEPTH = 256
VMEM_BYTES = 56 * 2**20

VMEM_SPEC = pl.BlockSpec(memory_space=pltpu.VMEM)
SMEM_SPEC = pl.BlockSpec(memory_space=pltpu.SMEM)
ANY_SPEC = pl.BlockSpec(memory_space=pl.ANY)


def dot(a, b, ca, cb, precision=None):
    return lax.dot_general(
        a, b, (((ca,), (cb,)), ((), ())), preferred_element_type=F32, precision=precision
    )


def params():
    return pltpu.CompilerParams(vmem_limit_bytes=VMEM_BYTES)


def exchange(pieces, axis):
    n = lax.axis_size(axis)
    return [
        lax.ppermute(pieces[m], axis, [(i, i ^ m) for i in range(n)]) for m in range(1, n)
    ]


def spread(value, axis):
    n = lax.axis_size(axis)
    return [value] + [
        lax.ppermute(value, axis, [(i, (i + s) % n) for i in range(n)]) for s in range(1, n)
    ]


def butterfly(value, axis):
    n = lax.axis_size(axis)
    step = 1
    while step < n:
        value = value + lax.ppermute(value, axis, [(i, i ^ step) for i in range(n)])
        step *= 2
    return value


class Sizes:
    def __init__(self, positions, start, send_list, pair_rows):
        self.blocks, self.comps, self.width = positions.shape
        self.vectors = start.shape[1]
        self.peers = lax.axis_size("cells")
        self.cols = lax.axis_size("cols")
        self.cap = send_list.shape[2]
        self.slots = self.peers * self.cap
        self.own = self.blocks // self.cols
        self.pairs = pair_rows.shape[2] * self.cols
        self.long = 2 * self.pairs + GROUP
        self.short = self.pairs + GROUP
        self.at0, self.at1 = 0, self.long
        self.ats = 2 * self.long
        self.at2 = self.ats + self.short
        self.head = self.at2 + self.short
        self.mine = self.head + 8
        self.theirs = self.mine + self.slots
        self.table = self.theirs + self.slots
        self.bundle = self.comps + self.vectors + 16


def divide(value, by):
    if by & (by - 1):
        return value // by
    return lax.shift_right_arithmetic(value, jnp.int32(by.bit_length() - 1))


def remainder(value, by):
    if by & (by - 1):
        return value % by
    return jnp.bitwise_and(value, jnp.int32(by - 1))


def build_table(sz, pairs, send_all, where):
    count = len(pairs)
    each = sz.pairs // sz.cols

    def kernel(*refs):
        pair_refs, (send_ref, where_ref, tab, slot_owner) = refs[:count], refs[count:]
        c = where_ref[0]
        z = where_ref[1]
        base = z * sz.own

        def lists(i, carry):
            m = divide(i, sz.cap)
            q = remainder(i, sz.cap)
            tab[sz.mine + i] = send_ref[0, jnp.bitwise_xor(c, m) * sz.cap + q]
            tab[sz.theirs + i] = send_ref[m, c * sz.cap + q]
            slot_owner[i] = divide(send_ref[m, c * sz.cap + q], sz.own)
            return carry

        lax.fori_loop(0, sz.slots, lists, 0)
        carry = (jnp.int32(0),) * 4
        for ref in pair_refs:

            def pair(i, carry, ref=ref):
                n0, n1, ns, n2 = carry
                r = ref[0, i]
                p = ref[1, i]
                local = p < sz.blocks
                row_mine = divide(r, sz.own) == z
                partner_mine = divide(p, sz.own) == z
                slot = jnp.maximum(p - sz.blocks, 0)
                slot = jnp.bitwise_xor(divide(slot, sz.cap), c) * sz.cap + remainder(slot, sz.cap)
                slot_mine = slot_owner[slot] == z
                forward = (r - base) * 256 + p
                back = (p - base) * 256 + r
                both = jnp.logical_and(row_mine, partner_mine)
                other = jnp.logical_and(local, row_mine != partner_mine)
                tab[sz.at0 + n0] = forward
                n0 = n0 + jnp.where(both, 1, 0)
                tab[sz.at0 + n0] = back
                n0 = n0 + jnp.where(jnp.logical_and(both, p != r), 1, 0)
                tab[sz.at1 + n1] = jnp.where(row_mine, forward, back)
                n1 = n1 + jnp.where(other, 1, 0)
                far = jnp.logical_not(local)
                tab[sz.at2 + n2] = (r - base) * 256 + slot
                n2 = n2 + jnp.where(jnp.logical_and(far, row_mine), 1, 0)
                tab[sz.ats + ns] = slot * 256 + r
                ns = ns + jnp.where(jnp.logical_and(far, slot_mine), 1, 0)
                return n0, n1, ns, n2

            carry = lax.fori_loop(0, each, pair, carry, unroll=4)
        n0, n1, ns, n2 = carry
        tab[sz.head] = z
        for k, (at, n, dummy) in enumerate(
            ((sz.at0, n0, sz.own), (sz.at1, n1, sz.own), (sz.ats, ns, sz.slots), (sz.at2, n2, sz.own))
        ):
            for i in range(GROUP):
                tab[at + n + i] = dummy * 256
            tab[sz.head + 1 + k] = divide(n + GROUP - 1, GROUP)
        for i in range(5, 8):
            tab[sz.head + i] = 0

    return pl.pallas_call(
        kernel,
        out_shape=jax.ShapeDtypeStruct((sz.table,), jnp.int32),
        in_specs=[SMEM_SPEC] * (count + 2),
        out_specs=SMEM_SPEC,
        scratch_shapes=[pltpu.SMEM((sz.slots,), jnp.int32)],
    )(*pairs, send_all, where)


def select_row(ref, b):
    value = ref[...].astype(F32)
    rows = lax.broadcasted_iota(jnp.int32, value.shape, 0)
    return jnp.sum(jnp.where(rows == b, value, 0.0), axis=0, keepdims=True)


def outgoing_blocks(sz, send, where, positions, scales, start):
    def kernel(send_ref, where_ref, points, spreads, vectors, *outs):
        c = where_ref[0]
        for m in range(1, sz.peers):
            for q in range(sz.cap):
                b = send_ref[0, jnp.bitwise_xor(c, m) * sz.cap + q]
                b = jnp.minimum(b, sz.blocks - 1)
                out = outs[m - 1]
                out[q, 0 : sz.comps] = points[b]
                out[q, sz.comps : sz.comps + sz.vectors] = vectors[b]
                row = jnp.broadcast_to(select_row(spreads, b), (16, sz.width))
                out[q, sz.comps + sz.vectors :] = row.astype(BF16)

    shape = jax.ShapeDtypeStruct((sz.cap, sz.bundle, sz.width), BF16)
    return pl.pallas_call(
        kernel,
        out_shape=(shape,) * (sz.peers - 1),
        in_specs=[SMEM_SPEC] * 2 + [VMEM_SPEC] * 3,
        out_specs=(VMEM_SPEC,) * (sz.peers - 1),
        compiler_params=params(),
    )(send, where, positions, scales, start)


def split3(value):
    first = value.astype(BF16)
    rest = value - first.astype(F32)
    second = rest.astype(BF16)
    third = (rest - second.astype(F32)).astype(BF16)
    return first, second, third


def fill_factors(points, spread_row, left, right):
    comps = points.shape[0]
    x = points.astype(F32)
    inverse = 1.0 / spread_row
    norms = jnp.sum(x * x, axis=0, keepdims=True)
    y = x * (inverse * math.sqrt(2.0 * LOG2E))
    high = y.astype(BF16)
    low = (y - high.astype(F32)).astype(BF16)
    a1, a2, a3 = split3(norms * inverse * LOG2E)
    b1, b2, b3 = split3(inverse)
    left[0:comps] = high
    left[comps : 2 * comps] = low
    left[2 * comps : 3 * comps] = high
    right[0:comps] = high
    right[comps : 2 * comps] = high
    right[2 * comps : 3 * comps] = low
    shape = (16, points.shape[1])
    row = lax.broadcasted_iota(jnp.int32, shape, 0)
    lefts = (-a1, -a1, -a2, -a2, -a1, -a3, -b1, -b2, -b1, -b2, -b3, -b1)
    rights = (b1, b2, b1, b2, b3, b1, a1, a1, a2, a2, a1, a3)
    l_rest = jnp.zeros(shape, F32)
    r_rest = jnp.zeros(shape, F32)
    for k, (l_row, r_row) in enumerate(zip(lefts, rights)):
        l_rest = jnp.where(row == k, l_row.astype(F32), l_rest)
        r_rest = jnp.where(row == k, r_row.astype(F32), r_rest)
    at = 3 * comps
    left[at : at + 16] = l_rest.astype(BF16)
    right[at : at + 16] = r_rest.astype(BF16)
    unused = jnp.zeros((DEPTH - at - 16, points.shape[1]), BF16)
    left[at + 16 :] = unused
    right[at + 16 :] = unused


def segments(sz, tab, name):
    g0, g1, gs, g2 = (tab[sz.head + 1 + k] for k in range(4))
    if name == "0":
        return sz.at0, g0, 0
    if name == "1":
        return sz.at1, g1, g0
    if name == "S":
        return sz.ats, gs, g0 + g1
    return sz.at2, g2, g0 + g1 + gs


def entry(tab, place):
    code = tab[place]
    return lax.shift_right_arithmetic(code, jnp.int32(8)), jnp.bitwise_and(code, jnp.int32(255))


def row_block(sz, tab, name, row):
    if name == "S":
        return sz.blocks + jnp.minimum(row, sz.slots - 1)
    return tab[sz.head] * sz.own + jnp.minimum(row, sz.own - 1)


def partner_block(sz, name, partner):
    return sz.blocks + partner if name == "2" else partner


def build_tiles(sz, table, names, positions, scales, bundles, earlier):
    first = earlier is None
    many = len(bundles)
    held = sz.blocks + (sz.slots if many else 0)
    sum_rows = sz.own + 1 + sz.slots + 1
    writes = 3

    def kernel(*refs):
        tab, points, spreads = refs[:3]
        bundle_refs, refs = refs[3 : 3 + many], refs[3 + many :]
        if first:
            store, sum_out, left, right, ring, sem = refs
            sums = sum_out
            sums[...] = jnp.zeros(sums.shape, F32)
        else:
            _, old, store, sum_out, left, right, ring, sem, sums = refs
            sums[...] = old[...]

        def local(b, carry):
            fill_factors(points[b], select_row(spreads, b), left.at[b], right.at[b])
            return carry

        lax.fori_loop(0, sz.blocks, local, 0)
        for m in range(1, many + 1):

            def far(q, carry, m=m):
                at = sz.blocks + m * sz.cap + q
                bundle = bundle_refs[m - 1]
                row = bundle[q, sz.comps + sz.vectors :][0:1].astype(F32)
                fill_factors(bundle[q, 0 : sz.comps], row, left.at[at], right.at[at])
                return carry

            lax.fori_loop(0, sz.cap, far, 0)

        def write(slot, step):
            return pltpu.make_async_copy(
                ring.at[slot], store.at[pl.ds(step * GROUP, GROUP)], sem.at[slot]
            )

        done = jnp.int32(0)
        for name in names:
            table_at, steps, place = segments(sz, tab, name)
            base = 0 if name != "S" else sz.own + 1

            def step(t, carry, name=name, table_at=table_at, place=place, base=base, done=done):
                slot = lax.rem(done + t, writes)

                @pl.when(done + t >= writes)
                def _():
                    write(slot, 0).wait()

                for k in range(GROUP):
                    row, partner = entry(tab, table_at + t * GROUP + k)
                    r = row_block(sz, tab, name, row)
                    p = partner_block(sz, name, partner)
                    kernel_tile = jnp.exp2(dot(left[p], right[r], 0, 0))
                    ring[slot, k] = kernel_tile.astype(BF16)
                    sums[base + row] += jnp.sum(
                        kernel_tile.reshape(sz.width // 8, 8, sz.width), axis=0
                    )
                write(slot, jnp.minimum(place + t, STORED // GROUP)).start()
                return carry

            lax.fori_loop(0, steps, step, 0)
            done = done + steps
        for slot in range(writes):

            @pl.when(done >= slot + 1)
            def _(slot=slot):
                write(slot, 0).wait()

        if not first:
            for row in range(sz.own):
                sum_out[row : row + 1] = jnp.sum(sums[row], axis=0, keepdims=True)
            for row in range(sz.slots):
                at = sz.own + row
                sum_out[at : at + 1] = jnp.sum(sums[at + 1], axis=0, keepdims=True)

    tile_shape = jax.ShapeDtypeStruct((STORED + GROUP, sz.width, sz.width), BF16)
    sums_shape = (sum_rows, 8, sz.width)
    args = [table, positions, scales, *bundles]
    specs = [SMEM_SPEC] + [VMEM_SPEC] * (2 + many)
    scratch = [
        pltpu.VMEM((held, DEPTH, sz.width), BF16),
        pltpu.VMEM((held, DEPTH, sz.width), BF16),
        pltpu.VMEM((writes, GROUP, sz.width, sz.width), BF16),
        pltpu.SemaphoreType.DMA((writes,)),
    ]
    aliases = {}
    if not first:
        aliases = {len(args): 0}
        args += list(earlier)
        specs += [ANY_SPEC, VMEM_SPEC]
        scratch.append(pltpu.VMEM(sums_shape, F32))
        sums_shape = (sz.own + sz.slots, sz.width)
    entries = 64 if first else 28
    return pl.pallas_call(
        kernel,
        out_shape=(tile_shape, jax.ShapeDtypeStruct(sums_shape, F32)),
        in_specs=specs,
        out_specs=(ANY_SPEC, VMEM_SPEC),
        scratch_shapes=scratch,
        input_output_aliases=aliases,
        compiler_params=params(),
        cost_estimate=pl.CostEstimate(
            flops=2 * entries * sz.width**2 * DEPTH,
            bytes_accessed=2 * entries * sz.width**2,
            transcendentals=entries * sz.width**2,
        ),
    )(*args)


def group_sums(sz, table, around):
    def kernel(tab, *refs):
        parts, out = refs[: sz.cols], refs[sz.cols]
        z = tab[sz.head]
        for s in range(sz.cols):
            owner = lax.rem(z - s + sz.cols, sz.cols)
            for b in range(sz.own):
                out[pl.ds(owner * sz.own + b, 1), :] = parts[s][b : b + 1]
        slots = parts[0][sz.own :]
        for s in range(1, sz.cols):
            slots += parts[s][sz.own :]
        out[sz.blocks :] = slots

    return pl.pallas_call(
        kernel,
        out_shape=jax.ShapeDtypeStruct((sz.blocks + sz.slots, sz.width), F32),
        in_specs=[SMEM_SPEC] + [VMEM_SPEC] * sz.cols,
        out_specs=VMEM_SPEC,
    )(table, *around)


def scale_start(sz, table, send_all, where, partial, start, bundles):
    def kernel(tab, send_ref, where_ref, *refs):
        parts = refs[: sz.peers]
        start_ref = refs[sz.peers]
        far_refs = refs[sz.peers + 1 : 2 * sz.peers]
        near_out, far_out, root_out, total = refs[2 * sz.peers :]
        c = where_ref[0]
        for m in range(sz.peers):
            total[m, 0 : sz.blocks] = parts[m][0 : sz.blocks]
        for m in range(sz.peers):
            for k in range(sz.peers):
                if k == m:
                    continue
                for q in range(sz.cap):
                    b = send_ref[m, jnp.bitwise_xor(c, k) * sz.cap + q]
                    at = sz.blocks + (k ^ m) * sz.cap + q
                    total[m, pl.ds(b, 1), :] += parts[k][at : at + 1, :]
        root = lax.rsqrt(total[0, 0 : sz.blocks])
        root_out[...] = root
        for b in range(sz.blocks):
            near_out[b] = (root[b : b + 1] * start_ref[b].astype(F32)).astype(BF16)
        far_out[0 : sz.cap] = jnp.zeros((sz.cap, sz.vectors, sz.width), BF16)
        for m in range(1, sz.peers):
            for q in range(sz.cap):
                b = jnp.minimum(tab[sz.theirs + m * sz.cap + q], sz.blocks - 1)
                far_root = lax.rsqrt(total[m, pl.ds(b, 1), :])
                far_out[m * sz.cap + q] = (far_root * far_refs[m - 1][q, sz.comps : sz.comps + sz.vectors].astype(F32)).astype(BF16)

    return pl.pallas_call(
        kernel,
        out_shape=(
            jax.ShapeDtypeStruct((sz.blocks, sz.vectors, sz.width), BF16),
            jax.ShapeDtypeStruct((sz.slots, sz.vectors, sz.width), BF16),
            jax.ShapeDtypeStruct((sz.blocks, sz.width), F32),
        ),
        in_specs=[SMEM_SPEC] * 3 + [VMEM_SPEC] * (2 * sz.peers),
        out_specs=(VMEM_SPEC,) * 3,
        scratch_shapes=[pltpu.VMEM((sz.peers, sz.blocks + 8, sz.width), F32)],
        compiler_params=params(),
    )(table, send_all, where, *partial, start, *bundles)


def sweep_scratch(sz, held):
    return [
        pltpu.VMEM((held, sz.vectors, sz.width), BF16),
        pltpu.VMEM((RING, GROUP, sz.width, sz.width), BF16),
        pltpu.SemaphoreType.DMA((RING,)),
        pltpu.SemaphoreType.DMA((max(sz.cols, sz.peers),)),
        pltpu.VMEM((sz.bundle, sz.width), BF16),
        pltpu.VMEM((2, DEPTH, sz.width), BF16),
        pltpu.SemaphoreType.DMA((1,)),
    ]


class Stream:
    def __init__(self, sz, tab, names, store, geometry, scratch):
        self.sz, self.tab, self.name, self.store, self.geometry = sz, tab, names[-1], store, geometry
        _, self.ring, self.sem, _, self.x, self.factors, self.xsem = scratch
        self.table_at, self.steps, self.place = segments(sz, tab, names[0])
        self.split = None
        if len(names) > 1:
            self.split = self.steps
            self.second_at, steps, _ = segments(sz, tab, names[1])
            self.steps = self.steps + steps

    def entries(self, t):
        if self.split is None:
            return self.table_at + t * GROUP
        after = self.second_at + (t - self.split) * GROUP
        return jnp.where(t < self.split, self.table_at + t * GROUP, after)

    def read(self, t):
        slot = lax.rem(t, RING)
        return pltpu.make_async_copy(
            self.store.at[pl.ds((self.place + t) * GROUP, GROUP)], self.ring.at[slot], self.sem.at[slot]
        )

    def stored(self, t):
        return jnp.logical_and(t < self.steps, self.place + t < STORED // GROUP)

    def begin(self):
        for t in range(RING - 1):

            @pl.when(self.stored(t))
            def _(t=t):
                self.read(t).start()

    def factors_of(self, place):
        sz = self.sz
        points, scales, bundles = self.geometry

        def fetch(source, rows):
            copy = pltpu.make_async_copy(source, self.x.at[pl.ds(0, rows)], self.xsem.at[0])
            copy.start()
            copy.wait()

        @pl.when(place < sz.blocks)
        def _():
            fetch(points.at[place], sz.comps)

        slot = place - sz.blocks
        for m in range(1, sz.peers):

            @pl.when(jnp.logical_and(slot >= m * sz.cap, slot < (m + 1) * sz.cap))
            def _(m=m):
                fetch(bundles[m - 1].at[slot - m * sz.cap], sz.bundle)

        far_row = self.x[sz.comps + sz.vectors :][0:1].astype(F32)
        row = jnp.where(place < sz.blocks, select_row(scales, place), far_row)
        fill_factors(self.x[0 : sz.comps], row, self.factors.at[0], self.factors.at[1])

    def rebuild(self, t):
        slot = lax.rem(t, RING)

        def one(k, carry):
            row, partner = entry(self.tab, self.entries(t) + k)
            self.factors_of(partner_block(self.sz, self.name, partner))
            left = self.factors[0]
            self.factors_of(row_block(self.sz, self.tab, self.name, row))
            self.ring[slot, k] = jnp.exp2(dot(left, self.factors[1], 0, 0)).astype(BF16)
            return carry

        lax.fori_loop(0, GROUP, one, 0)

    def run(self, vectors, target):
        def step(t, carry):
            ahead = t + RING - 1

            @pl.when(self.stored(ahead))
            def _():
                self.read(ahead).start()

            have = self.stored(t)

            @pl.when(have)
            def _():
                self.read(t).wait()

            @pl.when(jnp.logical_not(have))
            def _():
                self.rebuild(t)

            slot = lax.rem(t, RING)
            for k in range(GROUP):
                row, partner = entry(self.tab, self.entries(t) + k)
                target[row] += dot(vectors[partner], self.ring[slot, k], 1, 0)
            return carry

        lax.fori_loop(0, self.steps, step, 0)


def load_vectors(sz, tab, pieces, vbuf, sem):
    copies = []
    for s, piece in enumerate(pieces):
        if piece.shape[0] == sz.blocks and sz.cols > 1:
            target = vbuf
        else:
            owner = lax.rem(tab[sz.head] - s + sz.cols, sz.cols)
            target = vbuf.at[pl.ds(owner * sz.own, sz.own)]
        copies.append(pltpu.make_async_copy(piece, target, sem.at[s]))
    for copy in copies:
        copy.start()
    return copies


def sweep_cost(sz, entries):
    return pl.CostEstimate(
        flops=2 * entries * sz.width**2 * sz.vectors * 4,
        bytes_accessed=2 * entries * sz.width**2,
        transcendentals=0,
    )


def geometry_specs(sz):
    return [ANY_SPEC, VMEM_SPEC] + [ANY_SPEC] * (sz.peers - 1)


def split_geometry(sz, refs):
    return (refs[0], refs[1], refs[2 : sz.peers + 1]), refs[sz.peers + 1 :]


def slot_products(sz, table, tiles, geometry, pieces, inverse):
    count = len(pieces)
    others = sz.peers - 1
    with_picks = inverse is not None

    def kernel(tab, store, *refs):
        blocks, refs = split_geometry(sz, refs)
        if with_picks:
            inverse_ref, refs = refs[0], refs[1:]
        piece_refs, refs = refs[:count], refs[count:]
        outs, refs = refs[:others], refs[others:]
        if with_picks:
            picks, refs = refs[:others], refs[others:]
        total, refs = refs[0], refs[1:]
        stream = Stream(sz, tab, "S", store, blocks, refs)
        vbuf = refs[0]
        copies = load_vectors(sz, tab, piece_refs, vbuf, refs[3])
        stream.begin()
        total[...] = jnp.zeros(total.shape, F32)
        for copy in copies:
            copy.wait()
        if with_picks:
            for m in range(1, sz.peers):
                for q in range(sz.cap):
                    b = jnp.minimum(tab[sz.mine + m * sz.cap + q], sz.blocks - 1)
                    picks[m - 1][q] = vbuf[b]
        stream.run(vbuf, total)
        for m in range(1, sz.peers):
            for q in range(sz.cap):
                products = total[m * sz.cap + q]
                if with_picks:
                    products = dot(inverse_ref[...], products, 1, 0, lax.Precision.HIGHEST)
                outs[m - 1][q] = products.astype(BF16)

    dims = (sz.cap, sz.vectors, sz.width)
    shapes = (jax.ShapeDtypeStruct(dims, BF16),) * others
    args = [table, tiles, *geometry]
    specs = [SMEM_SPEC, ANY_SPEC] + geometry_specs(sz)
    if with_picks:
        shapes *= 2
        args.append(inverse)
        specs.append(VMEM_SPEC)
    return pl.pallas_call(
        kernel,
        out_shape=shapes,
        in_specs=specs + [ANY_SPEC] * count,
        out_specs=(VMEM_SPEC,) * len(shapes),
        scratch_shapes=[pltpu.VMEM((sz.slots + 1, sz.vectors, sz.width), F32)]
        + sweep_scratch(sz, sz.blocks),
        compiler_params=params(),
        cost_estimate=sweep_cost(sz, 12),
    )(*args, *pieces)


def local_products(sz, table, tiles, geometry, pieces, names, earlier):
    count = len(pieces)
    first = earlier is None

    def kernel(tab, store, *refs):
        blocks, refs = split_geometry(sz, refs)
        piece_refs, refs = refs[:count], refs[count:]
        if not first:
            summed, refs = refs[0], refs[1:]
        out, total, refs = refs[0], refs[1], refs[2:]
        stream = Stream(sz, tab, names, store, blocks, refs)
        vbuf = refs[0]
        copies = load_vectors(sz, tab, piece_refs, vbuf, refs[3])
        stream.begin()
        if first:
            total[...] = jnp.zeros(total.shape, F32)
        else:
            total[0 : sz.own] = summed[...]
        for copy in copies:
            copy.wait()
        stream.run(vbuf, total)
        out[...] = total[0 : sz.own]

    args = [table, tiles, *geometry, *pieces]
    specs = [SMEM_SPEC, ANY_SPEC] + geometry_specs(sz) + [ANY_SPEC] * count
    if not first:
        args.append(earlier)
        specs.append(VMEM_SPEC)
    return pl.pallas_call(
        kernel,
        out_shape=jax.ShapeDtypeStruct((sz.own, sz.vectors, sz.width), F32),
        in_specs=specs,
        out_specs=VMEM_SPEC,
        scratch_shapes=[pltpu.VMEM((sz.own + 1, sz.vectors, sz.width), F32)]
        + sweep_scratch(sz, sz.blocks),
        compiler_params=params(),
        cost_estimate=sweep_cost(sz, sum(dict(zip("01", (18, 44)))[name] for name in names)),
    )(*args)


def far_products(sz, table, tiles, geometry, summed, far, returned, root, inverse):
    cells_total = sz.blocks * sz.width * sz.peers
    last = inverse is not None
    many = len(far)

    def kernel(tab, store, *refs):
        blocks, refs = split_geometry(sz, refs)
        summed_ref, root_ref, refs = refs[0], refs[1], refs[2:]
        if last:
            inverse_ref, refs = refs[0], refs[1:]
        far_refs, refs = refs[:many], refs[many:]
        back_refs, refs = refs[: sz.peers - 1], refs[sz.peers - 1 :]
        out, gram_out, total, refs = refs[0], refs[1], refs[2], refs[3:]
        stream = Stream(sz, tab, "2", store, blocks, refs[:7])
        vbuf, sem = refs[0], refs[3]
        if many == 1:
            copies = [pltpu.make_async_copy(far_refs[0], vbuf, sem.at[0])]
        else:
            copies = [
                pltpu.make_async_copy(far_refs[m - 1], vbuf.at[pl.ds(m * sz.cap, sz.cap)], sem.at[m])
                for m in range(1, sz.peers)
            ]
        for copy in copies:
            copy.start()
        stream.begin()
        z = tab[sz.head]
        total[0 : sz.own] = summed_ref[...]
        back = refs[-1] if last else total
        if last:
            back[...] = jnp.zeros(back.shape, F32)
        for m in range(1, sz.peers):
            for q in range(sz.cap):
                b = tab[sz.mine + m * sz.cap + q]

                @pl.when(divide(b, sz.own) == z)
                def _(m=m, q=q, b=b):
                    back[b - z * sz.own] += back_refs[m - 1][q].astype(F32)

        for copy in copies:
            copy.wait()
        stream.run(vbuf, total)
        gram = jnp.zeros((sz.vectors, sz.vectors), F32)
        for b in range(sz.own):
            root_row = root_ref[pl.ds(z * sz.own + b, 1), :]
            mapped = root_row * total[b]
            if last:
                mapped = dot(inverse_ref[...], mapped, 1, 0, lax.Precision.HIGHEST)
                mapped += root_row * back[b]
                out[b] = mapped
            else:
                out[b] = (root_row * mapped).astype(BF16)
            gram += dot(mapped, mapped, 1, 1, lax.Precision.HIGHEST)
        gram_out[...] = gram / cells_total

    args = [table, tiles, *geometry, summed, root]
    specs = [SMEM_SPEC, ANY_SPEC] + geometry_specs(sz) + [VMEM_SPEC] * 2
    if last:
        args.append(inverse)
        specs.append(VMEM_SPEC)
    args += [*far, *returned]
    specs += [ANY_SPEC] * many + [VMEM_SPEC] * len(returned)
    return pl.pallas_call(
        kernel,
        out_shape=(
            jax.ShapeDtypeStruct((sz.own, sz.vectors, sz.width), F32 if last else BF16),
            jax.ShapeDtypeStruct((sz.vectors, sz.vectors), F32),
        ),
        in_specs=specs,
        out_specs=(VMEM_SPEC, VMEM_SPEC),
        scratch_shapes=[pltpu.VMEM((sz.own + 1, sz.vectors, sz.width), F32)]
        + sweep_scratch(sz, sz.slots)
        + [pltpu.VMEM((sz.own, sz.vectors, sz.width), F32)] * last,
        compiler_params=params(),
        cost_estimate=sweep_cost(sz, 20),
    )(*args)


def inverse_factor(gram):
    n = gram.shape[0]
    eye = (
        lax.broadcasted_iota(jnp.int32, (n, n), 0) == lax.broadcasted_iota(jnp.int32, (n, n), 1)
    ).astype(F32)
    whole = jnp.concatenate([gram, eye], axis=1)
    chunk = 8
    parts = [whole[i : i + chunk] for i in range(0, n, chunk)]
    row_ids = lax.broadcasted_iota(jnp.int32, (chunk, 1), 0)
    for k in range(n):
        at, inside = k // chunk, k % chunk
        row = parts[at][inside : inside + 1]
        pivot = row[:, k : k + 1]
        ratio = row / pivot
        for j in range(at, n // chunk):
            factor = parts[j][:, k : k + 1]
            if j == at:
                if inside == chunk - 1:
                    continue
                factor = jnp.where(row_ids > inside, factor, 0.0)
            parts[j] = parts[j] - factor * ratio
    out = []
    for j in range(n // chunk):
        diagonal = jnp.sum(
            parts[j][:, :n] * eye[j * chunk : (j + 1) * chunk], axis=1, keepdims=True
        )
        out.append(parts[j][:, n:] * lax.rsqrt(diagonal))
    return jnp.concatenate(out, axis=0)


def factor_call(sz, gram):
    def kernel(gram_ref, out):
        out[...] = inverse_factor(gram_ref[...])

    return pl.pallas_call(
        kernel,
        out_shape=jax.ShapeDtypeStruct((sz.vectors, sz.vectors), F32),
        in_specs=[VMEM_SPEC],
        out_specs=VMEM_SPEC,
    )(gram)


def normalize(sz, table, gram, mapped):
    share = sz.vectors // sz.cols

    def kernel(tab, gram_ref, mapped_ref, *refs):
        outs, buf = refs[: sz.cols], refs[sz.cols]
        inverse = inverse_factor(gram_ref[...])
        z = tab[sz.head]
        for b in range(sz.own):
            buf[...] = dot(inverse, mapped_ref[b], 1, 0, lax.Precision.HIGHEST)
            for s in range(sz.cols):
                to = lax.rem(z + s, sz.cols)
                outs[s][b] = buf[pl.ds(pl.multiple_of(to * share, share), share)].astype(BF16)

    return pl.pallas_call(
        kernel,
        out_shape=(jax.ShapeDtypeStruct((sz.own, share, sz.width), BF16),) * sz.cols,
        in_specs=[SMEM_SPEC, VMEM_SPEC, VMEM_SPEC],
        out_specs=(VMEM_SPEC,) * sz.cols,
        scratch_shapes=[pltpu.VMEM((sz.vectors, sz.width), F32)],
        compiler_params=params(),
    )(table, gram, mapped)


def assemble(sz, table, pieces):
    share = sz.vectors // sz.cols

    def kernel(tab, *refs):
        out = refs[-1]
        z = tab[sz.head]
        for s in range(sz.cols):
            owner = lax.rem(z - s + sz.cols, sz.cols)
            for b in range(sz.own):
                out[owner * sz.own + b] = refs[s][b].astype(F32)

    return pl.pallas_call(
        kernel,
        out_shape=jax.ShapeDtypeStruct((sz.blocks, share, sz.width), F32),
        in_specs=[SMEM_SPEC] + [VMEM_SPEC] * sz.cols,
        out_specs=VMEM_SPEC,
        compiler_params=params(),
    )(table, *pieces)


def body(positions, scales, start_vectors, send_list, pair_rows, pair_partner):
    sz = Sizes(positions, start_vectors, send_list, pair_rows)
    where = jnp.stack([lax.axis_index("cells"), lax.axis_index("cols")]).astype(jnp.int32)
    n = sz.cols

    pairs = spread(
        jnp.concatenate([pair_rows.reshape(1, -1), pair_partner.reshape(1, -1)], axis=0), "cols"
    )
    lists = send_list.reshape(1, -1)
    send_all = jnp.concatenate([lists] + exchange([lists] * sz.peers, "cells"), axis=0)
    outgoing = outgoing_blocks(sz, lists, where, positions, scales, start_vectors)
    bundles = exchange((None,) + tuple(outgoing), "cells")

    table = build_table(sz, pairs, send_all, where)
    built = build_tiles(sz, table, "01", positions, scales, [], None)
    tiles, sums = build_tiles(sz, table, "S2", positions, scales, bundles, built)
    geometry = (positions, scales, *bundles)

    partial = group_sums(sz, table, spread(sums, "cols"))
    partials = [partial] + exchange([partial] * sz.peers, "cells")
    near, far, root = scale_start(sz, table, send_all, where, partials, start_vectors, bundles)

    sent = slot_products(sz, table, tiles, geometry, [near], None)
    returned = exchange((None,) + tuple(sent), "cells")
    summed = local_products(sz, table, tiles, geometry, [near], "01", None)
    scaled, gram = far_products(
        sz, table, tiles, geometry, summed, [far], returned, root, None
    )

    pieces = spread(scaled, "cols")
    gram = butterfly(sum(spread(gram, "cols")), "cells")
    summed = local_products(sz, table, tiles, geometry, [scaled], "0", None)
    first_inverse = factor_call(sz, gram)
    pieces, summed, first_inverse = lax.optimization_barrier((pieces, summed, first_inverse))
    sent = slot_products(sz, table, tiles, geometry, pieces, first_inverse)
    sent, picks = sent[: sz.peers - 1], sent[sz.peers - 1 :]
    far_pieces = exchange((None,) + tuple(picks), "cells")
    returned = exchange((None,) + tuple(sent), "cells")
    summed = local_products(sz, table, tiles, geometry, pieces, "1", summed)
    mapped, gram = far_products(
        sz, table, tiles, geometry, summed, far_pieces, returned, root, first_inverse
    )
    gram = butterfly(butterfly(gram, "cells"), "cols")
    shares = normalize(sz, table, gram, mapped)
    arrived = [shares[0]] + [
        lax.ppermute(shares[s], "cols", [(i, (i + s) % n) for i in range(n)]) for s in range(1, n)
    ]
    return assemble(sz, table, arrived)


def solution(mesh):
    in_specs = (
        P(("lineage", "cells"), None, None),
        P(("lineage", "cells"), None),
        P(("lineage", "cells"), None, None),
        P(("lineage", "cells"), None, None),
        P(("lineage", "cells"), "cols", None),
        P(("lineage", "cells"), "cols", None),
    )
    out_specs = P(("lineage", "cells"), "cols", None)
    return jax.shard_map(body, mesh=mesh, in_specs=in_specs, out_specs=out_specs, check_vma=False)
```

```python
import math

import jax
import jax.numpy as jnp
from jax import lax
from jax.experimental import pallas as pl
from jax.experimental.pallas import tpu as pltpu
from jax.sharding import PartitionSpec as P

F32 = jnp.float32
BF16 = jnp.bfloat16
LOG2E = math.log2(math.e)
MIB = 2**20
GROUP = 4
RING = 5
HBM_STEPS = (22, 11)
DEPTH = 256
VMEM_TOTAL = 60 * MIB

VMEM_SPEC = pl.BlockSpec(memory_space=pltpu.VMEM)
SMEM_SPEC = pl.BlockSpec(memory_space=pltpu.SMEM)
ANY_SPEC = pl.BlockSpec(memory_space=pl.ANY)
HBM_SPEC = pl.BlockSpec(memory_space=pltpu.HBM)


def dot(a, b, ca, cb, precision=None):
    return lax.dot_general(
        a, b, (((ca,), (cb,)), ((), ())), preferred_element_type=F32, precision=precision
    )


def params(limit):
    return pltpu.CompilerParams(vmem_limit_bytes=limit)


def exchange(pieces, axis):
    n = lax.axis_size(axis)
    return [
        lax.ppermute(pieces[m], axis, [(i, i ^ m) for i in range(n)]) for m in range(1, n)
    ]


def spread(value, axis):
    n = lax.axis_size(axis)
    return [value] + [
        lax.ppermute(value, axis, [(i, (i + s) % n) for i in range(n)]) for s in range(1, n)
    ]


def butterfly(value, axis):
    n = lax.axis_size(axis)
    step = 1
    while step < n:
        value = value + lax.ppermute(value, axis, [(i, i ^ step) for i in range(n)])
        step *= 2
    return value


class Sizes:
    def __init__(self, positions, start, send_list, pair_rows):
        self.blocks, self.comps, self.width = positions.shape
        self.vectors = start.shape[1]
        self.peers = lax.axis_size("cells")
        self.cols = lax.axis_size("cols")
        self.cap = send_list.shape[2]
        self.slots = self.peers * self.cap
        self.own = self.blocks // self.cols
        self.pairs = pair_rows.shape[2] * self.cols
        self.long = 2 * self.pairs + GROUP
        self.short = self.pairs + GROUP
        self.at0, self.at1 = 0, self.long
        self.ats = 2 * self.long
        self.at2 = self.ats + self.short
        self.head = self.at2 + self.short
        self.mine = self.head + 8
        self.theirs = self.mine + self.slots
        self.table = self.theirs + self.slots
        self.bundle = self.comps + self.vectors + 16
        factors = 2 * DEPTH * self.width * (self.blocks + self.own + 2 * self.slots)
        step = 2 * GROUP * self.width * self.width
        inputs = 2 * self.width * (self.blocks * self.comps + self.slots * self.bundle)
        self.limit = 16 * MIB + max(self.slots - 8, 0) * MIB
        self.build_bytes = factors + 2 * step + inputs + 3 * MIB
        steps = (VMEM_TOTAL - max(self.build_bytes, self.limit)) // step
        self.vmem_steps = (9, 4) if steps > 13 else (max(steps - 2, 1), 1)


def divide(value, by):
    if by & (by - 1):
        return value // by
    return lax.shift_right_arithmetic(value, jnp.int32(by.bit_length() - 1))


def remainder(value, by):
    if by & (by - 1):
        return value % by
    return jnp.bitwise_and(value, jnp.int32(by - 1))


def build_table(sz, pairs, send_all, where):
    count = len(pairs)
    each = sz.pairs // sz.cols
    batch = math.gcd(each, 8)

    def kernel(*refs):
        pair_refs, (send_ref, where_ref, tab, slot_owner) = refs[:count], refs[count:]
        c = where_ref[0]
        z = where_ref[1]
        base = z * sz.own

        def lists(i, carry):
            m = divide(i, sz.cap)
            q = remainder(i, sz.cap)
            tab[sz.mine + i] = send_ref[0, jnp.bitwise_xor(c, m) * sz.cap + q]
            tab[sz.theirs + i] = send_ref[m, c * sz.cap + q]
            slot_owner[i] = divide(send_ref[m, c * sz.cap + q], sz.own)
            return carry

        lax.fori_loop(0, sz.slots, lists, 0)
        carry = (jnp.int32(0),) * 4
        for ref in pair_refs:

            def some(i, carry, ref=ref):
                loaded = []
                for k in range(batch):
                    r = ref[0, i * batch + k]
                    p = ref[1, i * batch + k]
                    slot = jnp.maximum(p - sz.blocks, 0)
                    slot = jnp.bitwise_xor(divide(slot, sz.cap), c) * sz.cap + remainder(slot, sz.cap)
                    loaded.append((r, p, slot, slot_owner[slot] == z))
                for values in loaded:
                    carry = pair(values, carry)
                return carry

            def pair(values, carry):
                n0, n1, ns, n2 = carry
                r, p, slot, slot_mine = values
                local = p < sz.blocks
                row_mine = divide(r, sz.own) == z
                partner_mine = divide(p, sz.own) == z
                forward = (r - base) * 256 + p
                back = (p - base) * 256 + r
                both = jnp.logical_and(row_mine, partner_mine)
                other = jnp.logical_and(local, row_mine != partner_mine)
                tab[sz.at0 + n0] = forward
                n0 = n0 + jnp.where(both, 1, 0)
                tab[sz.at0 + n0] = back
                n0 = n0 + jnp.where(jnp.logical_and(both, p != r), 1, 0)
                tab[sz.at1 + n1] = jnp.where(row_mine, forward, back)
                n1 = n1 + jnp.where(other, 1, 0)
                far = jnp.logical_not(local)
                tab[sz.at2 + n2] = (r - base) * 256 + slot
                n2 = n2 + jnp.where(jnp.logical_and(far, row_mine), 1, 0)
                tab[sz.ats + ns] = slot * 256 + r
                ns = ns + jnp.where(jnp.logical_and(far, slot_mine), 1, 0)
                return n0, n1, ns, n2

            carry = lax.fori_loop(0, each // batch, some, carry)
        n0, n1, ns, n2 = carry
        tab[sz.head] = z
        for k, (at, n, dummy) in enumerate(
            ((sz.at0, n0, sz.own), (sz.at1, n1, sz.own), (sz.ats, ns, sz.slots), (sz.at2, n2, sz.own))
        ):
            for i in range(GROUP):
                tab[at + n + i] = dummy * 256
            tab[sz.head + 1 + k] = divide(n + GROUP - 1, GROUP)
        for i in range(5, 8):
            tab[sz.head + i] = 0

    return pl.pallas_call(
        kernel,
        out_shape=jax.ShapeDtypeStruct((sz.table,), jnp.int32),
        in_specs=[SMEM_SPEC] * (count + 2),
        out_specs=SMEM_SPEC,
        scratch_shapes=[pltpu.SMEM((sz.slots,), jnp.int32)],
        compiler_params=params(sz.limit),
    )(*pairs, send_all, where)


def select_row(ref, b):
    value = ref[...].astype(F32)
    rows = lax.broadcasted_iota(jnp.int32, value.shape, 0)
    return jnp.sum(jnp.where(rows == b, value, 0.0), axis=0, keepdims=True)


def outgoing_blocks(sz, send, where, positions, scales, start):
    def kernel(send_ref, where_ref, points, spreads, vectors, *outs):
        c = where_ref[0]
        for m in range(1, sz.peers):
            for q in range(sz.cap):
                b = send_ref[0, jnp.bitwise_xor(c, m) * sz.cap + q]
                b = jnp.minimum(b, sz.blocks - 1)
                out = outs[m - 1]
                out[q, 0 : sz.comps] = points[b]
                out[q, sz.comps : sz.comps + sz.vectors] = vectors[b]
                row = jnp.broadcast_to(select_row(spreads, b), (16, sz.width))
                out[q, sz.comps + sz.vectors :] = row.astype(BF16)

    shape = jax.ShapeDtypeStruct((sz.cap, sz.bundle, sz.width), BF16)
    return pl.pallas_call(
        kernel,
        out_shape=(shape,) * (sz.peers - 1),
        in_specs=[SMEM_SPEC] * 2 + [VMEM_SPEC] * 3,
        out_specs=(VMEM_SPEC,) * (sz.peers - 1),
        compiler_params=params(sz.limit),
    )(send, where, positions, scales, start)


def split3(value):
    first = value.astype(BF16)
    rest = value - first.astype(F32)
    second = rest.astype(BF16)
    third = (rest - second.astype(F32)).astype(BF16)
    return first, second, third


def fill_factors(points, spread_row, left, right):
    comps, width = points.shape
    x = points.astype(F32)
    inverse = 1.0 / spread_row
    norms = jnp.sum(x * x, axis=0, keepdims=True)
    y = x * (inverse * math.sqrt(2.0 * LOG2E))
    high = y.astype(BF16)
    low = (y - high.astype(F32)).astype(BF16)
    a1, a2, a3 = split3(norms * inverse * LOG2E)
    b1, b2, b3 = split3(inverse)
    lefts = (-a1, -a1, -a2, -a2, -a1, -a3, -b1, -b2, -b1, -b2, -b3, -b1)
    rights = (b1, b2, b1, b2, b3, b1, a1, a1, a2, a2, a1, a3)
    row = lax.broadcasted_iota(jnp.int32, (16, width), 0)
    at = 3 * comps
    for ref, parts, rest in ((left, (high, low, high), lefts), (right, (high, high, low), rights)):
        if ref is None:
            continue
        for k, part in enumerate(parts):
            ref[k * comps : (k + 1) * comps] = part
        block = jnp.zeros((16, width), F32)
        for k, value in enumerate(rest):
            block = jnp.where(row == k, value.astype(F32), block)
        ref[at : at + 16] = block.astype(BF16)
        ref[at + 16 :] = jnp.zeros((DEPTH - at - 16, width), BF16)


def segments(sz, tab, name):
    g0, g1, gs, g2 = (tab[sz.head + 1 + k] for k in range(4))
    return {
        "0": (sz.at0, g0, 0),
        "1": (sz.at1, g1, g0),
        "S": (sz.ats, gs, 0),
        "2": (sz.at2, g2, gs),
    }[name]


def in_vmem(sz, name, place, steps):
    held = sz.vmem_steps[name in "S2"]
    return jnp.clip(held - place, 0, steps), held


def entry(tab, place):
    code = tab[place]
    return lax.shift_right_arithmetic(code, jnp.int32(8)), jnp.bitwise_and(code, jnp.int32(255))


def row_block(sz, tab, name, row):
    if name == "S":
        return sz.blocks + jnp.minimum(row, sz.slots - 1)
    return tab[sz.head] * sz.own + jnp.minimum(row, sz.own - 1)


def partner_block(sz, name, partner):
    return sz.blocks + partner if name == "2" else partner


def build_tiles(sz, table, names, positions, scales, bundles, earlier):
    first = earlier is None
    many = len(bundles)
    sum_rows = sz.own + 1 + sz.slots + 1
    writes = 2
    held = sz.vmem_steps[not first]
    stored = HBM_STEPS[not first]
    offset = 0 if first else HBM_STEPS[0] + 1

    def kernel(*refs):
        tab, points, spreads = refs[:3]
        bundle_refs, refs = refs[3 : 3 + many], refs[3 + many :]
        if first:
            kept, store, sum_out, left, right, ring, sem = refs
            sums = sum_out
            sums[...] = jnp.zeros(sums.shape, F32)
        else:
            _, old, kept, store, sum_out, left, right, ring, sem, sums = refs
            sums[...] = old[...]
        z = tab[sz.head]

        def local(b, carry):
            fill_factors(points[b], select_row(spreads, b), left.at[b], None)
            return carry

        def own(i, carry):
            b = z * sz.own + i
            fill_factors(points[b], select_row(spreads, b), None, right.at[i])
            return carry

        lax.fori_loop(0, sz.blocks, local, 0)
        lax.fori_loop(0, sz.own, own, 0)
        for m in range(1, many + 1):

            def far(q, carry, m=m):
                slot = m * sz.cap + q
                bundle = bundle_refs[m - 1]
                row = bundle[q, sz.comps + sz.vectors :][0:1].astype(F32)
                fill_factors(
                    bundle[q, 0 : sz.comps], row, left.at[sz.blocks + slot], right.at[sz.own + slot]
                )
                return carry

            lax.fori_loop(0, sz.cap, far, 0)

        def write(slot, step):
            return pltpu.make_async_copy(
                ring.at[slot], store.at[pl.ds(step * GROUP, GROUP)], sem.at[slot]
            )

        done = jnp.int32(0)
        for name in names:
            table_at, steps, place = segments(sz, tab, name)
            near, _ = in_vmem(sz, name, place, steps)

            def tiles(t, target, name=name, table_at=table_at):
                for k in range(GROUP):
                    row, partner = entry(tab, table_at + t * GROUP + k)
                    if name == "S":
                        r = sz.own + jnp.minimum(row, sz.slots - 1)
                        row = row + sz.own + 1
                    else:
                        r = jnp.minimum(row, sz.own - 1)
                    p = partner_block(sz, name, partner)
                    kernel_tile = jnp.exp2(dot(left[p], right[r], 0, 0))
                    target(k, kernel_tile.astype(BF16))
                    sums[row] += jnp.sum(kernel_tile.reshape(sz.width // 8, 8, sz.width), axis=0)

            def keep(t, carry, place=place, tiles=tiles):
                def put(k, tile):
                    kept[(place + t) * GROUP + k] = tile

                tiles(t, put)
                return carry

            def send(t, carry, place=place, tiles=tiles, near=near, done=done):
                u = done + t - near
                slot = lax.rem(u, writes)

                @pl.when(u >= writes)
                def _():
                    write(slot, 0).wait()

                def put(k, tile):
                    ring[slot, k] = tile

                tiles(t, put)
                write(slot, offset + jnp.minimum(place + t - held, stored)).start()
                return carry

            lax.fori_loop(0, near, keep, 0)
            lax.fori_loop(near, steps, send, 0)
            done = done + steps - near
        for slot in range(writes):

            @pl.when(done >= slot + 1)
            def _(slot=slot):
                write(slot, 0).wait()

        if not first:
            for row in range(sz.own):
                sum_out[row : row + 1] = jnp.sum(sums[row], axis=0, keepdims=True)
            for row in range(sz.slots):
                at = sz.own + row
                sum_out[at : at + 1] = jnp.sum(sums[at + 1], axis=0, keepdims=True)

    tile = (sz.width, sz.width)
    sums_shape = (sum_rows, 8, sz.width)
    args = [table, positions, scales, *bundles]
    specs = [SMEM_SPEC] + [VMEM_SPEC] * (2 + many)
    scratch = [
        pltpu.VMEM((sz.blocks + (0 if first else sz.slots), DEPTH, sz.width), BF16),
        pltpu.VMEM((sz.own + (0 if first else sz.slots), DEPTH, sz.width), BF16),
        pltpu.VMEM((writes, GROUP) + tile, BF16),
        pltpu.SemaphoreType.DMA((writes,)),
    ]
    aliases = {}
    if not first:
        aliases = {len(args): 1}
        args += list(earlier)
        specs += [HBM_SPEC, VMEM_SPEC]
        scratch.append(pltpu.VMEM(sums_shape, F32))
        sums_shape = (sz.own + sz.slots, sz.width)
    entries = 64 if first else 28
    return pl.pallas_call(
        kernel,
        out_shape=(
            pltpu.VMEM((held * GROUP,) + tile, BF16),
            pltpu.HBM(((sum(HBM_STEPS) + 2) * GROUP,) + tile, BF16),
            jax.ShapeDtypeStruct(sums_shape, F32),
        ),
        in_specs=specs,
        out_specs=(VMEM_SPEC, HBM_SPEC, VMEM_SPEC),
        scratch_shapes=scratch,
        input_output_aliases=aliases,
        compiler_params=params(max(sz.build_bytes, sz.limit)),
        cost_estimate=pl.CostEstimate(
            flops=2 * entries * sz.width**2 * DEPTH,
            bytes_accessed=2 * entries * sz.width**2,
            transcendentals=entries * sz.width**2,
        ),
    )(*args)


def group_sums(sz, table, around):
    def kernel(tab, *refs):
        parts, out = refs[: sz.cols], refs[sz.cols]
        z = tab[sz.head]
        for s in range(sz.cols):
            owner = lax.rem(z - s + sz.cols, sz.cols)
            for b in range(sz.own):
                out[pl.ds(owner * sz.own + b, 1), :] = parts[s][b : b + 1]
        slots = parts[0][sz.own :]
        for s in range(1, sz.cols):
            slots += parts[s][sz.own :]
        out[sz.blocks :] = slots

    return pl.pallas_call(
        kernel,
        out_shape=jax.ShapeDtypeStruct((sz.blocks + sz.slots, sz.width), F32),
        in_specs=[SMEM_SPEC] + [VMEM_SPEC] * sz.cols,
        out_specs=VMEM_SPEC,
        compiler_params=params(sz.limit),
    )(table, *around)


def scale_start(sz, table, send_all, where, partial, start, bundles):
    def kernel(tab, send_ref, where_ref, *refs):
        parts = refs[: sz.peers]
        start_ref = refs[sz.peers]
        far_refs = refs[sz.peers + 1 : 2 * sz.peers]
        near_out, far_out, root_out, total = refs[2 * sz.peers :]
        c = where_ref[0]
        for m in range(sz.peers):
            total[m, 0 : sz.blocks] = parts[m][0 : sz.blocks]
        for m in range(sz.peers):
            for k in range(sz.peers):
                if k == m:
                    continue
                for q in range(sz.cap):
                    b = send_ref[m, jnp.bitwise_xor(c, k) * sz.cap + q]
                    at = sz.blocks + (k ^ m) * sz.cap + q
                    total[m, pl.ds(b, 1), :] += parts[k][at : at + 1, :]
        root = lax.rsqrt(total[0, 0 : sz.blocks])
        root_out[...] = root
        for b in range(sz.blocks):
            near_out[b] = (root[b : b + 1] * start_ref[b].astype(F32)).astype(BF16)
        far_out[0 : sz.cap] = jnp.zeros((sz.cap, sz.vectors, sz.width), BF16)
        for m in range(1, sz.peers):
            for q in range(sz.cap):
                b = jnp.minimum(tab[sz.theirs + m * sz.cap + q], sz.blocks - 1)
                far_root = lax.rsqrt(total[m, pl.ds(b, 1), :])
                far_out[m * sz.cap + q] = (far_root * far_refs[m - 1][q, sz.comps : sz.comps + sz.vectors].astype(F32)).astype(BF16)

    return pl.pallas_call(
        kernel,
        out_shape=(
            jax.ShapeDtypeStruct((sz.blocks, sz.vectors, sz.width), BF16),
            jax.ShapeDtypeStruct((sz.slots, sz.vectors, sz.width), BF16),
            jax.ShapeDtypeStruct((sz.blocks, sz.width), F32),
        ),
        in_specs=[SMEM_SPEC] * 3 + [VMEM_SPEC] * (2 * sz.peers),
        out_specs=(VMEM_SPEC,) * 3,
        scratch_shapes=[pltpu.VMEM((sz.peers, sz.blocks + 8, sz.width), F32)],
        compiler_params=params(sz.limit),
    )(table, send_all, where, *partial, start, *bundles)


def sweep_scratch(sz, held):
    return [
        pltpu.VMEM((held, sz.vectors, sz.width), BF16),
        pltpu.VMEM((RING, GROUP, sz.width, sz.width), BF16),
        pltpu.SemaphoreType.DMA((RING,)),
        pltpu.SemaphoreType.DMA((max(sz.cols, sz.peers),)),
        pltpu.VMEM((sz.bundle, sz.width), BF16),
        pltpu.VMEM((2, DEPTH, sz.width), BF16),
        pltpu.SemaphoreType.DMA((1,)),
    ]


class Stream:
    def __init__(self, sz, tab, names, tiles, geometry, scratch):
        self.sz, self.tab, self.name, self.geometry = sz, tab, names[-1], geometry
        self.kept, self.store = tiles
        _, self.ring, self.sem, _, self.x, self.factors, self.xsem = scratch
        self.table_at, self.steps, self.place = segments(sz, tab, names[0])
        self.split = None
        if len(names) > 1:
            self.split = self.steps
            self.second_at, steps, _ = segments(sz, tab, names[1])
            self.steps = self.steps + steps
        self.near, self.held = in_vmem(sz, self.name, self.place, self.steps)
        self.limit = HBM_STEPS[self.name in "S2"]
        self.offset = HBM_STEPS[0] + 1 if self.name in "S2" else 0

    def entries(self, t):
        if self.split is None:
            return self.table_at + t * GROUP
        after = self.second_at + (t - self.split) * GROUP
        return jnp.where(t < self.split, self.table_at + t * GROUP, after)

    def slot(self, t):
        return lax.rem(t - self.near, RING)

    def read(self, t):
        place = self.offset + self.place + t - self.held
        return pltpu.make_async_copy(
            self.store.at[pl.ds(place * GROUP, GROUP)], self.ring.at[self.slot(t)], self.sem.at[self.slot(t)]
        )

    def stored(self, t):
        return jnp.logical_and(t < self.steps, self.place + t - self.held < self.limit)

    def begin(self):
        for k in range(RING - 1):

            @pl.when(self.stored(self.near + k))
            def _(k=k):
                self.read(self.near + k).start()

    def factors_of(self, place):
        sz = self.sz
        points, scales, bundles = self.geometry

        def fetch(source, rows):
            copy = pltpu.make_async_copy(source, self.x.at[pl.ds(0, rows)], self.xsem.at[0])
            copy.start()
            copy.wait()

        @pl.when(place < sz.blocks)
        def _():
            fetch(points.at[place], sz.comps)

        slot = place - sz.blocks
        for m in range(1, sz.peers):

            @pl.when(jnp.logical_and(slot >= m * sz.cap, slot < (m + 1) * sz.cap))
            def _(m=m):
                fetch(bundles[m - 1].at[slot - m * sz.cap], sz.bundle)

        far_row = self.x[sz.comps + sz.vectors :][0:1].astype(F32)
        row = jnp.where(place < sz.blocks, select_row(scales, place), far_row)
        fill_factors(self.x[0 : sz.comps], row, self.factors.at[0], self.factors.at[1])

    def rebuild(self, t):
        slot = self.slot(t)

        def one(k, carry):
            row, partner = entry(self.tab, self.entries(t) + k)
            self.factors_of(partner_block(self.sz, self.name, partner))
            left = self.factors[0]
            self.factors_of(row_block(self.sz, self.tab, self.name, row))
            self.ring[slot, k] = jnp.exp2(dot(left, self.factors[1], 0, 0)).astype(BF16)
            return carry

        lax.fori_loop(0, GROUP, one, 0)

    def run(self, vectors, target):
        def products(t, tile):
            for k in range(GROUP):
                row, partner = entry(self.tab, self.entries(t) + k)
                target[row] += dot(vectors[partner], tile(k), 1, 0)

        def near(t, carry):
            products(t, lambda k: self.kept[(self.place + t) * GROUP + k])
            return carry

        def step(t, carry):
            ahead = t + RING - 1

            @pl.when(self.stored(ahead))
            def _():
                self.read(ahead).start()

            have = self.stored(t)

            @pl.when(have)
            def _():
                self.read(t).wait()

            @pl.when(jnp.logical_not(have))
            def _():
                self.rebuild(t)

            products(t, lambda k: self.ring[self.slot(t), k])
            return carry

        lax.fori_loop(0, self.near, near, 0)
        lax.fori_loop(self.near, self.steps, step, 0)


def load_vectors(sz, tab, pieces, vbuf, sem):
    copies = []
    for s, piece in enumerate(pieces):
        if piece.shape[0] == sz.blocks and sz.cols > 1:
            target = vbuf
        else:
            owner = lax.rem(tab[sz.head] - s + sz.cols, sz.cols)
            target = vbuf.at[pl.ds(owner * sz.own, sz.own)]
        copies.append(pltpu.make_async_copy(piece, target, sem.at[s]))
    for copy in copies:
        copy.start()
    return copies


def sweep_cost(sz, entries):
    return pl.CostEstimate(
        flops=2 * entries * sz.width**2 * sz.vectors * 4,
        bytes_accessed=2 * entries * sz.width**2,
        transcendentals=0,
    )


def geometry_specs(sz):
    return [ANY_SPEC, VMEM_SPEC] + [ANY_SPEC] * (sz.peers - 1)


def split_geometry(sz, refs):
    return (refs[0], refs[1], refs[2 : sz.peers + 1]), refs[sz.peers + 1 :]


def slot_products(sz, table, tiles, geometry, pieces, inverse):
    count = len(pieces)
    others = sz.peers - 1
    with_picks = inverse is not None

    def kernel(tab, kept, store, *refs):
        blocks, refs = split_geometry(sz, refs)
        if with_picks:
            inverse_ref, refs = refs[0], refs[1:]
        piece_refs, refs = refs[:count], refs[count:]
        outs, refs = refs[:others], refs[others:]
        if with_picks:
            picks, refs = refs[:others], refs[others:]
        total, refs = refs[0], refs[1:]
        stream = Stream(sz, tab, "S", (kept, store), blocks, refs)
        vbuf = refs[0]
        copies = load_vectors(sz, tab, piece_refs, vbuf, refs[3])
        stream.begin()
        total[...] = jnp.zeros(total.shape, F32)
        for copy in copies:
            copy.wait()
        if with_picks:
            for m in range(1, sz.peers):
                for q in range(sz.cap):
                    b = jnp.minimum(tab[sz.mine + m * sz.cap + q], sz.blocks - 1)
                    picks[m - 1][q] = vbuf[b]
        stream.run(vbuf, total)
        for m in range(1, sz.peers):
            for q in range(sz.cap):
                products = total[m * sz.cap + q]
                if with_picks:
                    products = dot(inverse_ref[...], products, 1, 0, lax.Precision.HIGHEST)
                outs[m - 1][q] = products.astype(BF16)

    dims = (sz.cap, sz.vectors, sz.width)
    shapes = (jax.ShapeDtypeStruct(dims, BF16),) * others
    args = [table, *tiles, *geometry]
    specs = [SMEM_SPEC, VMEM_SPEC, HBM_SPEC] + geometry_specs(sz)
    if with_picks:
        shapes *= 2
        args.append(inverse)
        specs.append(VMEM_SPEC)
    return pl.pallas_call(
        kernel,
        out_shape=shapes,
        in_specs=specs + [ANY_SPEC] * count,
        out_specs=(VMEM_SPEC,) * len(shapes),
        scratch_shapes=[pltpu.VMEM((sz.slots + 1, sz.vectors, sz.width), F32)]
        + sweep_scratch(sz, sz.blocks),
        compiler_params=params(sz.limit),
        cost_estimate=sweep_cost(sz, 12),
    )(*args, *pieces)


def local_products(sz, table, tiles, geometry, pieces, names, earlier):
    count = len(pieces)
    first = earlier is None

    def kernel(tab, kept, store, *refs):
        blocks, refs = split_geometry(sz, refs)
        piece_refs, refs = refs[:count], refs[count:]
        if not first:
            summed, refs = refs[0], refs[1:]
        out, total, refs = refs[0], refs[1], refs[2:]
        stream = Stream(sz, tab, names, (kept, store), blocks, refs)
        vbuf = refs[0]
        copies = load_vectors(sz, tab, piece_refs, vbuf, refs[3])
        stream.begin()
        if first:
            total[...] = jnp.zeros(total.shape, F32)
        else:
            total[0 : sz.own] = summed[...]
        for copy in copies:
            copy.wait()
        stream.run(vbuf, total)
        out[...] = total[0 : sz.own]

    args = [table, *tiles, *geometry, *pieces]
    specs = [SMEM_SPEC, VMEM_SPEC, HBM_SPEC] + geometry_specs(sz) + [ANY_SPEC] * count
    if not first:
        args.append(earlier)
        specs.append(VMEM_SPEC)
    return pl.pallas_call(
        kernel,
        out_shape=jax.ShapeDtypeStruct((sz.own, sz.vectors, sz.width), F32),
        in_specs=specs,
        out_specs=VMEM_SPEC,
        scratch_shapes=[pltpu.VMEM((sz.own + 1, sz.vectors, sz.width), F32)]
        + sweep_scratch(sz, sz.blocks),
        compiler_params=params(sz.limit),
        cost_estimate=sweep_cost(sz, sum(dict(zip("01", (18, 44)))[name] for name in names)),
    )(*args)


def far_products(sz, table, tiles, geometry, summed, far, returned, root, inverse):
    cells_total = sz.blocks * sz.width * sz.peers
    last = inverse is not None
    many = len(far)

    def kernel(tab, kept, store, *refs):
        blocks, refs = split_geometry(sz, refs)
        summed_ref, root_ref, refs = refs[0], refs[1], refs[2:]
        if last:
            inverse_ref, refs = refs[0], refs[1:]
        far_refs, refs = refs[:many], refs[many:]
        back_refs, refs = refs[: sz.peers - 1], refs[sz.peers - 1 :]
        out, gram_out, total, refs = refs[0], refs[1], refs[2], refs[3:]
        stream = Stream(sz, tab, "2", (kept, store), blocks, refs[:7])
        vbuf, sem = refs[0], refs[3]
        if many == 1:
            copies = [pltpu.make_async_copy(far_refs[0], vbuf, sem.at[0])]
        else:
            copies = [
                pltpu.make_async_copy(far_refs[m - 1], vbuf.at[pl.ds(m * sz.cap, sz.cap)], sem.at[m])
                for m in range(1, sz.peers)
            ]
        for copy in copies:
            copy.start()
        stream.begin()
        z = tab[sz.head]
        total[0 : sz.own] = summed_ref[...]
        back = refs[-1] if last else total
        if last:
            back[...] = jnp.zeros(back.shape, F32)
        for m in range(1, sz.peers):
            for q in range(sz.cap):
                b = tab[sz.mine + m * sz.cap + q]

                @pl.when(divide(b, sz.own) == z)
                def _(m=m, q=q, b=b):
                    back[b - z * sz.own] += back_refs[m - 1][q].astype(F32)

        for copy in copies:
            copy.wait()
        stream.run(vbuf, total)
        gram = jnp.zeros((sz.vectors, sz.vectors), F32)
        for b in range(sz.own):
            root_row = root_ref[pl.ds(z * sz.own + b, 1), :]
            mapped = root_row * total[b]
            if last:
                mapped = dot(inverse_ref[...], mapped, 1, 0, lax.Precision.HIGHEST)
                mapped += root_row * back[b]
                out[b] = mapped
            else:
                out[b] = (root_row * mapped).astype(BF16)
            gram += dot(mapped, mapped, 1, 1, lax.Precision.HIGHEST)
        gram_out[...] = gram / cells_total

    args = [table, *tiles, *geometry, summed, root]
    specs = [SMEM_SPEC, VMEM_SPEC, HBM_SPEC] + geometry_specs(sz) + [VMEM_SPEC] * 2
    if last:
        args.append(inverse)
        specs.append(VMEM_SPEC)
    args += [*far, *returned]
    specs += [ANY_SPEC] * many + [VMEM_SPEC] * len(returned)
    return pl.pallas_call(
        kernel,
        out_shape=(
            jax.ShapeDtypeStruct((sz.own, sz.vectors, sz.width), F32 if last else BF16),
            jax.ShapeDtypeStruct((sz.vectors, sz.vectors), F32),
        ),
        in_specs=specs,
        out_specs=(VMEM_SPEC, VMEM_SPEC),
        scratch_shapes=[pltpu.VMEM((sz.own + 1, sz.vectors, sz.width), F32)]
        + sweep_scratch(sz, sz.slots)
        + [pltpu.VMEM((sz.own, sz.vectors, sz.width), F32)] * last,
        compiler_params=params(sz.limit),
        cost_estimate=sweep_cost(sz, 20),
    )(*args)


def inverse_factor(gram):
    n = gram.shape[0]
    eye = (
        lax.broadcasted_iota(jnp.int32, (n, n), 0) == lax.broadcasted_iota(jnp.int32, (n, n), 1)
    ).astype(F32)
    whole = jnp.concatenate([gram, eye], axis=1)
    chunk = 8
    parts = [whole[i : i + chunk] for i in range(0, n, chunk)]
    row_ids = lax.broadcasted_iota(jnp.int32, (chunk, 1), 0)
    for k in range(n):
        at, inside = k // chunk, k % chunk
        row = parts[at][inside : inside + 1]
        pivot = row[:, k : k + 1]
        ratio = row / pivot
        for j in range(at, n // chunk):
            factor = parts[j][:, k : k + 1]
            if j == at:
                if inside == chunk - 1:
                    continue
                factor = jnp.where(row_ids > inside, factor, 0.0)
            parts[j] = parts[j] - factor * ratio
    out = []
    for j in range(n // chunk):
        diagonal = jnp.sum(
            parts[j][:, :n] * eye[j * chunk : (j + 1) * chunk], axis=1, keepdims=True
        )
        out.append(parts[j][:, n:] * lax.rsqrt(diagonal))
    return jnp.concatenate(out, axis=0)


def factor_call(sz, gram):
    def kernel(gram_ref, out):
        out[...] = inverse_factor(gram_ref[...])

    return pl.pallas_call(
        kernel,
        out_shape=jax.ShapeDtypeStruct((sz.vectors, sz.vectors), F32),
        in_specs=[VMEM_SPEC],
        out_specs=VMEM_SPEC,
        compiler_params=params(sz.limit),
    )(gram)


def normalize(sz, table, gram, mapped):
    share = sz.vectors // sz.cols

    def kernel(tab, gram_ref, mapped_ref, *refs):
        outs, buf = refs[: sz.cols], refs[sz.cols]
        inverse = inverse_factor(gram_ref[...])
        z = tab[sz.head]
        for b in range(sz.own):
            buf[...] = dot(inverse, mapped_ref[b], 1, 0, lax.Precision.HIGHEST)
            for s in range(sz.cols):
                to = lax.rem(z + s, sz.cols)
                outs[s][b] = buf[pl.ds(pl.multiple_of(to * share, share), share)].astype(BF16)

    return pl.pallas_call(
        kernel,
        out_shape=(jax.ShapeDtypeStruct((sz.own, share, sz.width), BF16),) * sz.cols,
        in_specs=[SMEM_SPEC, VMEM_SPEC, VMEM_SPEC],
        out_specs=(VMEM_SPEC,) * sz.cols,
        scratch_shapes=[pltpu.VMEM((sz.vectors, sz.width), F32)],
        compiler_params=params(sz.limit),
    )(table, gram, mapped)


def assemble(sz, table, pieces):
    share = sz.vectors // sz.cols

    def kernel(tab, *refs):
        out = refs[-1]
        z = tab[sz.head]
        for s in range(sz.cols):
            owner = lax.rem(z - s + sz.cols, sz.cols)
            for b in range(sz.own):
                out[owner * sz.own + b] = refs[s][b].astype(F32)

    return pl.pallas_call(
        kernel,
        out_shape=jax.ShapeDtypeStruct((sz.blocks, share, sz.width), F32),
        in_specs=[SMEM_SPEC] + [VMEM_SPEC] * sz.cols,
        out_specs=VMEM_SPEC,
        compiler_params=params(sz.limit),
    )(table, *pieces)


def body(positions, scales, start_vectors, send_list, pair_rows, pair_partner):
    sz = Sizes(positions, start_vectors, send_list, pair_rows)
    where = jnp.stack([lax.axis_index("cells"), lax.axis_index("cols")]).astype(jnp.int32)
    n = sz.cols

    pairs = spread(
        jnp.concatenate([pair_rows.reshape(1, -1), pair_partner.reshape(1, -1)], axis=0), "cols"
    )
    lists = send_list.reshape(1, -1)
    send_all = jnp.concatenate([lists] + exchange([lists] * sz.peers, "cells"), axis=0)
    outgoing = outgoing_blocks(sz, lists, where, positions, scales, start_vectors)
    bundles = exchange((None,) + tuple(outgoing), "cells")

    table = build_table(sz, pairs, send_all, where)
    near_kept, *earlier = build_tiles(sz, table, "01", positions, scales, [], None)
    far_kept, store, sums = build_tiles(sz, table, "S2", positions, scales, bundles, earlier)
    near_tiles, far_tiles = (near_kept, store), (far_kept, store)
    geometry = (positions, scales, *bundles)

    partial = group_sums(sz, table, spread(sums, "cols"))
    partials = [partial] + exchange([partial] * sz.peers, "cells")
    near, far, root = scale_start(sz, table, send_all, where, partials, start_vectors, bundles)

    sent = slot_products(sz, table, far_tiles, geometry, [near], None)
    returned = exchange((None,) + tuple(sent), "cells")
    summed = local_products(sz, table, near_tiles, geometry, [near], "01", None)
    scaled, gram = far_products(
        sz, table, far_tiles, geometry, summed, [far], returned, root, None
    )

    pieces = spread(scaled, "cols")
    gram = butterfly(sum(spread(gram, "cols")), "cells")
    summed = local_products(sz, table, near_tiles, geometry, [scaled], "0", None)
    first_inverse = factor_call(sz, gram)
    pieces, summed, first_inverse = lax.optimization_barrier((pieces, summed, first_inverse))
    sent = slot_products(sz, table, far_tiles, geometry, pieces, first_inverse)
    sent, picks = sent[: sz.peers - 1], sent[sz.peers - 1 :]
    far_pieces = exchange((None,) + tuple(picks), "cells")
    returned = exchange((None,) + tuple(sent), "cells")
    summed = local_products(sz, table, near_tiles, geometry, pieces, "1", summed)
    mapped, gram = far_products(
        sz, table, far_tiles, geometry, summed, far_pieces, returned, root, first_inverse
    )
    gram = butterfly(butterfly(gram, "cells"), "cols")
    shares = normalize(sz, table, gram, mapped)
    arrived = [shares[0]] + [
        lax.ppermute(shares[s], "cols", [(i, (i + s) % n) for i in range(n)]) for s in range(1, n)
    ]
    return assemble(sz, table, arrived)


def solution(mesh):
    in_specs = (
        P(("lineage", "cells"), None, None),
        P(("lineage", "cells"), None),
        P(("lineage", "cells"), None, None),
        P(("lineage", "cells"), None, None),
        P(("lineage", "cells"), "cols", None),
        P(("lineage", "cells"), "cols", None),
    )
    out_specs = P(("lineage", "cells"), "cols", None)
    return jax.shard_map(body, mesh=mesh, in_specs=in_specs, out_specs=out_specs, check_vma=False)
```

```python
import math

import jax
import jax.numpy as jnp
from jax import lax
from jax.experimental import pallas as pl
from jax.experimental.pallas import tpu as pltpu
from jax.sharding import PartitionSpec as P

F32 = jnp.float32
BF16 = jnp.bfloat16
LOG2E = math.log2(math.e)
MIB = 2**20
GROUP = 4
RING = 5
HBM_STEPS = (22, 11)
DEPTH = 256
VMEM_TOTAL = 60 * MIB

VMEM_SPEC = pl.BlockSpec(memory_space=pltpu.VMEM)
SMEM_SPEC = pl.BlockSpec(memory_space=pltpu.SMEM)
ANY_SPEC = pl.BlockSpec(memory_space=pl.ANY)
HBM_SPEC = pl.BlockSpec(memory_space=pltpu.HBM)


def dot(a, b, ca, cb, precision=None):
    return lax.dot_general(
        a, b, (((ca,), (cb,)), ((), ())), preferred_element_type=F32, precision=precision
    )


def params(limit):
    return pltpu.CompilerParams(vmem_limit_bytes=limit)


def exchange(pieces, axis):
    n = lax.axis_size(axis)
    return [
        lax.ppermute(pieces[m], axis, [(i, i ^ m) for i in range(n)]) for m in range(1, n)
    ]


def spread(value, axis):
    n = lax.axis_size(axis)
    return [value] + [
        lax.ppermute(value, axis, [(i, (i + s) % n) for i in range(n)]) for s in range(1, n)
    ]


def butterfly(value, axis):
    n = lax.axis_size(axis)
    step = 1
    while step < n:
        value = value + lax.ppermute(value, axis, [(i, i ^ step) for i in range(n)])
        step *= 2
    return value


class Sizes:
    def __init__(self, positions, start, send_list, pair_rows):
        self.blocks, self.comps, self.width = positions.shape
        self.vectors = start.shape[1]
        self.peers = lax.axis_size("cells")
        self.cols = lax.axis_size("cols")
        self.cap = send_list.shape[2]
        self.slots = self.peers * self.cap
        self.own = self.blocks // self.cols
        self.pairs = pair_rows.shape[2] * self.cols
        self.long = 2 * self.pairs + GROUP
        self.short = self.pairs + GROUP
        self.at0, self.at1 = 0, self.long
        self.ats = 2 * self.long
        self.at2 = self.ats + self.short
        self.head = self.at2 + self.short
        self.mine = self.head + 8
        self.theirs = self.mine + self.slots
        self.table = self.theirs + self.slots
        self.bundle = self.comps + self.vectors + 16
        factors = 2 * DEPTH * self.width * (self.blocks + self.own + 2 * self.slots)
        step = 2 * GROUP * self.width * self.width
        inputs = 2 * self.width * (self.blocks * self.comps + self.slots * self.bundle)
        self.limit = 16 * MIB + max(self.slots - 8, 0) * MIB
        self.build_bytes = factors + 2 * step + inputs + 3 * MIB
        steps = (VMEM_TOTAL - max(self.build_bytes, self.limit)) // step
        self.vmem_steps = (9, 4) if steps > 13 else (max(steps - 2, 1), 1)


def divide(value, by):
    if by & (by - 1):
        return value // by
    return lax.shift_right_arithmetic(value, jnp.int32(by.bit_length() - 1))


def remainder(value, by):
    if by & (by - 1):
        return value % by
    return jnp.bitwise_and(value, jnp.int32(by - 1))


def build_table(sz, pairs, send_all, where):
    count = len(pairs)
    each = sz.pairs // sz.cols
    batch = math.gcd(each, 8)

    def kernel(*refs):
        pair_refs, (send_ref, where_ref, tab, slot_owner) = refs[:count], refs[count:]
        c = where_ref[0]
        z = where_ref[1]
        base = z * sz.own

        def lists(i, carry):
            m = divide(i, sz.cap)
            q = remainder(i, sz.cap)
            tab[sz.mine + i] = send_ref[0, jnp.bitwise_xor(c, m) * sz.cap + q]
            tab[sz.theirs + i] = send_ref[m, c * sz.cap + q]
            slot_owner[i] = divide(send_ref[m, c * sz.cap + q], sz.own)
            return carry

        lax.fori_loop(0, sz.slots, lists, 0)
        carry = (jnp.int32(0),) * 4
        for ref in pair_refs:

            def some(i, carry, ref=ref):
                loaded = []
                for k in range(batch):
                    r = ref[0, i * batch + k]
                    p = ref[1, i * batch + k]
                    slot = jnp.maximum(p - sz.blocks, 0)
                    slot = jnp.bitwise_xor(divide(slot, sz.cap), c) * sz.cap + remainder(slot, sz.cap)
                    loaded.append((r, p, slot, slot_owner[slot] == z))
                for values in loaded:
                    carry = pair(values, carry)
                return carry

            def pair(values, carry):
                n0, n1, ns, n2 = carry
                r, p, slot, slot_mine = values
                local = p < sz.blocks
                row_mine = divide(r, sz.own) == z
                partner_mine = divide(p, sz.own) == z
                forward = (r - base) * 256 + p
                back = (p - base) * 256 + r
                both = jnp.logical_and(row_mine, partner_mine)
                other = jnp.logical_and(local, row_mine != partner_mine)
                tab[sz.at0 + n0] = forward
                n0 = n0 + jnp.where(both, 1, 0)
                tab[sz.at0 + n0] = back
                n0 = n0 + jnp.where(jnp.logical_and(both, p != r), 1, 0)
                tab[sz.at1 + n1] = jnp.where(row_mine, forward, back)
                n1 = n1 + jnp.where(other, 1, 0)
                far = jnp.logical_not(local)
                tab[sz.at2 + n2] = (r - base) * 256 + slot
                n2 = n2 + jnp.where(jnp.logical_and(far, row_mine), 1, 0)
                tab[sz.ats + ns] = slot * 256 + r
                ns = ns + jnp.where(jnp.logical_and(far, slot_mine), 1, 0)
                return n0, n1, ns, n2

            carry = lax.fori_loop(0, each // batch, some, carry)
        n0, n1, ns, n2 = carry
        tab[sz.head] = z
        for k, (at, n, dummy) in enumerate(
            ((sz.at0, n0, sz.own), (sz.at1, n1, sz.own), (sz.ats, ns, sz.slots), (sz.at2, n2, sz.own))
        ):
            for i in range(GROUP):
                tab[at + n + i] = dummy * 256
            tab[sz.head + 1 + k] = divide(n + GROUP - 1, GROUP)
        for i in range(5, 8):
            tab[sz.head + i] = 0

    return pl.pallas_call(
        kernel,
        out_shape=jax.ShapeDtypeStruct((sz.table,), jnp.int32),
        in_specs=[SMEM_SPEC] * (count + 2),
        out_specs=SMEM_SPEC,
        scratch_shapes=[pltpu.SMEM((sz.slots,), jnp.int32)],
        compiler_params=params(sz.limit),
    )(*pairs, send_all, where)


def select_row(ref, b):
    value = ref[...].astype(F32)
    rows = lax.broadcasted_iota(jnp.int32, value.shape, 0)
    return jnp.sum(jnp.where(rows == b, value, 0.0), axis=0, keepdims=True)


def outgoing_blocks(sz, send, where, positions, scales, start):
    def kernel(send_ref, where_ref, points, spreads, vectors, *outs):
        c = where_ref[0]
        for m in range(1, sz.peers):
            for q in range(sz.cap):
                b = send_ref[0, jnp.bitwise_xor(c, m) * sz.cap + q]
                b = jnp.minimum(b, sz.blocks - 1)
                out = outs[m - 1]
                out[q, 0 : sz.comps] = points[b]
                out[q, sz.comps : sz.comps + sz.vectors] = vectors[b]
                row = jnp.broadcast_to(select_row(spreads, b), (16, sz.width))
                out[q, sz.comps + sz.vectors :] = row.astype(BF16)

    shape = jax.ShapeDtypeStruct((sz.cap, sz.bundle, sz.width), BF16)
    return pl.pallas_call(
        kernel,
        out_shape=(shape,) * (sz.peers - 1),
        in_specs=[SMEM_SPEC] * 2 + [VMEM_SPEC] * 3,
        out_specs=(VMEM_SPEC,) * (sz.peers - 1),
        compiler_params=params(sz.limit),
    )(send, where, positions, scales, start)


def split3(value):
    first = value.astype(BF16)
    rest = value - first.astype(F32)
    second = rest.astype(BF16)
    third = (rest - second.astype(F32)).astype(BF16)
    return first, second, third


def fill_factors(points, spread_row, left, right):
    comps, width = points.shape
    x = points.astype(F32)
    inverse = 1.0 / spread_row
    norms = jnp.sum(x * x, axis=0, keepdims=True)
    y = x * (inverse * math.sqrt(2.0 * LOG2E))
    high = y.astype(BF16)
    low = (y - high.astype(F32)).astype(BF16)
    a1, a2, a3 = split3(norms * inverse * LOG2E)
    b1, b2, b3 = split3(inverse)
    lefts = (-a1, -a1, -a2, -a2, -a1, -a3, -b1, -b2, -b1, -b2, -b3, -b1)
    rights = (b1, b2, b1, b2, b3, b1, a1, a1, a2, a2, a1, a3)
    row = lax.broadcasted_iota(jnp.int32, (16, width), 0)
    at = 3 * comps
    for ref, parts, rest in ((left, (high, low, high), lefts), (right, (high, high, low), rights)):
        if ref is None:
            continue
        for k, part in enumerate(parts):
            ref[k * comps : (k + 1) * comps] = part
        block = jnp.zeros((16, width), F32)
        for k, value in enumerate(rest):
            block = jnp.where(row == k, value.astype(F32), block)
        ref[at : at + 16] = block.astype(BF16)
        ref[at + 16 :] = jnp.zeros((DEPTH - at - 16, width), BF16)


def segments(sz, tab, name):
    g0, g1, gs, g2 = (tab[sz.head + 1 + k] for k in range(4))
    return {
        "0": (sz.at0, g0, 0),
        "1": (sz.at1, g1, g0),
        "S": (sz.ats, gs, 0),
        "2": (sz.at2, g2, gs),
    }[name]


def in_vmem(sz, name, place, steps):
    held = sz.vmem_steps[name in "S2"]
    return jnp.clip(held - place, 0, steps), held


def entry(tab, place):
    code = tab[place]
    return lax.shift_right_arithmetic(code, jnp.int32(8)), jnp.bitwise_and(code, jnp.int32(255))


def row_block(sz, tab, name, row):
    if name == "S":
        return sz.blocks + jnp.minimum(row, sz.slots - 1)
    return tab[sz.head] * sz.own + jnp.minimum(row, sz.own - 1)


def partner_block(sz, name, partner):
    return sz.blocks + partner if name == "2" else partner


def build_tiles(sz, table, names, positions, scales, bundles, earlier):
    first = earlier is None
    many = len(bundles)
    sum_rows = sz.own + 1 + sz.slots + 1
    writes = 3 if first else 2
    held = sz.vmem_steps[not first]
    stored = HBM_STEPS[not first]
    offset = 0 if first else HBM_STEPS[0] + 1

    def kernel(*refs):
        tab, points, spreads = refs[:3]
        bundle_refs, refs = refs[3 : 3 + many], refs[3 + many :]
        if first:
            kept, store, sum_out, left, right, ring, sem = refs
            sums = sum_out
            sums[...] = jnp.zeros(sums.shape, F32)
        else:
            _, old, kept, store, sum_out, left, right, ring, sem, sums = refs
            sums[...] = old[...]
        z = tab[sz.head]

        def local(b, carry):
            fill_factors(points[b], select_row(spreads, b), left.at[b], None)
            return carry

        def own(i, carry):
            b = z * sz.own + i
            fill_factors(points[b], select_row(spreads, b), None, right.at[i])
            return carry

        lax.fori_loop(0, sz.blocks, local, 0, unroll=4)
        lax.fori_loop(0, sz.own, own, 0, unroll=2)
        for m in range(1, many + 1):

            def far(q, carry, m=m):
                slot = m * sz.cap + q
                bundle = bundle_refs[m - 1]
                row = bundle[q, sz.comps + sz.vectors :][0:1].astype(F32)
                fill_factors(
                    bundle[q, 0 : sz.comps], row, left.at[sz.blocks + slot], right.at[sz.own + slot]
                )
                return carry

            lax.fori_loop(0, sz.cap, far, 0, unroll=2)

        def write(slot, step):
            return pltpu.make_async_copy(
                ring.at[slot], store.at[pl.ds(step * GROUP, GROUP)], sem.at[slot]
            )

        done = jnp.int32(0)
        for name in names:
            table_at, steps, place = segments(sz, tab, name)
            near, _ = in_vmem(sz, name, place, steps)

            def tiles(t, target, name=name, table_at=table_at):
                for k in range(GROUP):
                    row, partner = entry(tab, table_at + t * GROUP + k)
                    if name == "S":
                        r = sz.own + jnp.minimum(row, sz.slots - 1)
                        row = row + sz.own + 1
                    else:
                        r = jnp.minimum(row, sz.own - 1)
                    p = partner_block(sz, name, partner)
                    kernel_tile = jnp.exp2(dot(left[p], right[r], 0, 0))
                    target(k, kernel_tile.astype(BF16))
                    sums[row] += jnp.sum(kernel_tile.reshape(sz.width // 8, 8, sz.width), axis=0)

            def keep(t, carry, place=place, tiles=tiles):
                def put(k, tile):
                    kept[(place + t) * GROUP + k] = tile

                tiles(t, put)
                return carry

            def send(t, carry, place=place, tiles=tiles, near=near, done=done):
                u = done + t - near
                slot = lax.rem(u, writes)

                @pl.when(u >= writes)
                def _():
                    write(slot, 0).wait()

                def put(k, tile):
                    ring[slot, k] = tile

                tiles(t, put)
                write(slot, offset + jnp.minimum(place + t - held, stored)).start()
                return carry

            lax.fori_loop(0, near, keep, 0)
            lax.fori_loop(near, steps, send, 0)
            done = done + steps - near
        for slot in range(writes):

            @pl.when(done >= slot + 1)
            def _(slot=slot):
                write(slot, 0).wait()

        if not first:
            for row in range(sz.own):
                sum_out[row : row + 1] = jnp.sum(sums[row], axis=0, keepdims=True)
            for row in range(sz.slots):
                at = sz.own + row
                sum_out[at : at + 1] = jnp.sum(sums[at + 1], axis=0, keepdims=True)

    tile = (sz.width, sz.width)
    sums_shape = (sum_rows, 8, sz.width)
    args = [table, positions, scales, *bundles]
    specs = [SMEM_SPEC] + [VMEM_SPEC] * (2 + many)
    scratch = [
        pltpu.VMEM((sz.blocks + (0 if first else sz.slots), DEPTH, sz.width), BF16),
        pltpu.VMEM((sz.own + (0 if first else sz.slots), DEPTH, sz.width), BF16),
        pltpu.VMEM((writes, GROUP) + tile, BF16),
        pltpu.SemaphoreType.DMA((writes,)),
    ]
    aliases = {}
    if not first:
        aliases = {len(args): 1}
        args += list(earlier)
        specs += [HBM_SPEC, VMEM_SPEC]
        scratch.append(pltpu.VMEM(sums_shape, F32))
        sums_shape = (sz.own + sz.slots, sz.width)
    entries = 64 if first else 28
    return pl.pallas_call(
        kernel,
        out_shape=(
            pltpu.VMEM((held * GROUP,) + tile, BF16),
            pltpu.HBM(((sum(HBM_STEPS) + 2) * GROUP,) + tile, BF16),
            jax.ShapeDtypeStruct(sums_shape, F32),
        ),
        in_specs=specs,
        out_specs=(VMEM_SPEC, HBM_SPEC, VMEM_SPEC),
        scratch_shapes=scratch,
        input_output_aliases=aliases,
        compiler_params=params(max(sz.build_bytes, sz.limit)),
        cost_estimate=pl.CostEstimate(
            flops=2 * entries * sz.width**2 * DEPTH,
            bytes_accessed=2 * entries * sz.width**2,
            transcendentals=entries * sz.width**2,
        ),
    )(*args)


def group_sums(sz, table, around):
    def kernel(tab, *refs):
        parts, out = refs[: sz.cols], refs[sz.cols]
        z = tab[sz.head]
        for s in range(sz.cols):
            owner = lax.rem(z - s + sz.cols, sz.cols)
            for b in range(sz.own):
                out[pl.ds(owner * sz.own + b, 1), :] = parts[s][b : b + 1]
        slots = parts[0][sz.own :]
        for s in range(1, sz.cols):
            slots += parts[s][sz.own :]
        out[sz.blocks :] = slots

    return pl.pallas_call(
        kernel,
        out_shape=jax.ShapeDtypeStruct((sz.blocks + sz.slots, sz.width), F32),
        in_specs=[SMEM_SPEC] + [VMEM_SPEC] * sz.cols,
        out_specs=VMEM_SPEC,
        compiler_params=params(sz.limit),
    )(table, *around)


def scale_start(sz, table, send_all, where, partial, start, bundles):
    def kernel(tab, send_ref, where_ref, *refs):
        parts = refs[: sz.peers]
        start_ref = refs[sz.peers]
        far_refs = refs[sz.peers + 1 : 2 * sz.peers]
        near_out, far_out, root_out, total = refs[2 * sz.peers :]
        c = where_ref[0]
        for m in range(sz.peers):
            total[m, 0 : sz.blocks] = parts[m][0 : sz.blocks]
        for m in range(sz.peers):
            for k in range(sz.peers):
                if k == m:
                    continue
                for q in range(sz.cap):
                    b = send_ref[m, jnp.bitwise_xor(c, k) * sz.cap + q]
                    at = sz.blocks + (k ^ m) * sz.cap + q
                    total[m, pl.ds(b, 1), :] += parts[k][at : at + 1, :]
        root = lax.rsqrt(total[0, 0 : sz.blocks])
        root_out[...] = root
        for b in range(sz.blocks):
            near_out[b] = (root[b : b + 1] * start_ref[b].astype(F32)).astype(BF16)
        far_out[0 : sz.cap] = jnp.zeros((sz.cap, sz.vectors, sz.width), BF16)
        for m in range(1, sz.peers):
            for q in range(sz.cap):
                b = jnp.minimum(tab[sz.theirs + m * sz.cap + q], sz.blocks - 1)
                far_root = lax.rsqrt(total[m, pl.ds(b, 1), :])
                far_out[m * sz.cap + q] = (far_root * far_refs[m - 1][q, sz.comps : sz.comps + sz.vectors].astype(F32)).astype(BF16)

    return pl.pallas_call(
        kernel,
        out_shape=(
            jax.ShapeDtypeStruct((sz.blocks, sz.vectors, sz.width), BF16),
            jax.ShapeDtypeStruct((sz.slots, sz.vectors, sz.width), BF16),
            jax.ShapeDtypeStruct((sz.blocks, sz.width), F32),
        ),
        in_specs=[SMEM_SPEC] * 3 + [VMEM_SPEC] * (2 * sz.peers),
        out_specs=(VMEM_SPEC,) * 3,
        scratch_shapes=[pltpu.VMEM((sz.peers, sz.blocks + 8, sz.width), F32)],
        compiler_params=params(sz.limit),
    )(table, send_all, where, *partial, start, *bundles)


def sweep_scratch(sz, held):
    return [
        pltpu.VMEM((held, sz.vectors, sz.width), BF16),
        pltpu.VMEM((RING, GROUP, sz.width, sz.width), BF16),
        pltpu.SemaphoreType.DMA((RING,)),
        pltpu.SemaphoreType.DMA((max(sz.cols, sz.peers),)),
        pltpu.VMEM((sz.bundle, sz.width), BF16),
        pltpu.VMEM((2, DEPTH, sz.width), BF16),
        pltpu.SemaphoreType.DMA((1,)),
    ]


class Stream:
    def __init__(self, sz, tab, names, tiles, geometry, scratch):
        self.sz, self.tab, self.name, self.geometry = sz, tab, names[-1], geometry
        self.kept, self.store = tiles
        _, self.ring, self.sem, _, self.x, self.factors, self.xsem = scratch
        self.table_at, self.steps, self.place = segments(sz, tab, names[0])
        self.split = None
        if len(names) > 1:
            self.split = self.steps
            self.second_at, steps, _ = segments(sz, tab, names[1])
            self.steps = self.steps + steps
        self.near, self.held = in_vmem(sz, self.name, self.place, self.steps)
        self.limit = HBM_STEPS[self.name in "S2"]
        self.offset = HBM_STEPS[0] + 1 if self.name in "S2" else 0

    def entries(self, t):
        if self.split is None:
            return self.table_at + t * GROUP
        after = self.second_at + (t - self.split) * GROUP
        return jnp.where(t < self.split, self.table_at + t * GROUP, after)

    def slot(self, t):
        return lax.rem(t - self.near, RING)

    def read(self, t):
        place = self.offset + self.place + t - self.held
        return pltpu.make_async_copy(
            self.store.at[pl.ds(place * GROUP, GROUP)], self.ring.at[self.slot(t)], self.sem.at[self.slot(t)]
        )

    def stored(self, t):
        return jnp.logical_and(t < self.steps, self.place + t - self.held < self.limit)

    def begin(self):
        for k in range(RING - 1):

            @pl.when(self.stored(self.near + k))
            def _(k=k):
                self.read(self.near + k).start()

    def factors_of(self, place):
        sz = self.sz
        points, scales, bundles = self.geometry

        def fetch(source, rows):
            copy = pltpu.make_async_copy(source, self.x.at[pl.ds(0, rows)], self.xsem.at[0])
            copy.start()
            copy.wait()

        @pl.when(place < sz.blocks)
        def _():
            fetch(points.at[place], sz.comps)

        slot = place - sz.blocks
        for m in range(1, sz.peers):

            @pl.when(jnp.logical_and(slot >= m * sz.cap, slot < (m + 1) * sz.cap))
            def _(m=m):
                fetch(bundles[m - 1].at[slot - m * sz.cap], sz.bundle)

        far_row = self.x[sz.comps + sz.vectors :][0:1].astype(F32)
        row = jnp.where(place < sz.blocks, select_row(scales, place), far_row)
        fill_factors(self.x[0 : sz.comps], row, self.factors.at[0], self.factors.at[1])

    def rebuild(self, t):
        slot = self.slot(t)

        def one(k, carry):
            row, partner = entry(self.tab, self.entries(t) + k)
            self.factors_of(partner_block(self.sz, self.name, partner))
            left = self.factors[0]
            self.factors_of(row_block(self.sz, self.tab, self.name, row))
            self.ring[slot, k] = jnp.exp2(dot(left, self.factors[1], 0, 0)).astype(BF16)
            return carry

        lax.fori_loop(0, GROUP, one, 0)

    def run(self, vectors, target):
        def products(t, tile):
            for k in range(GROUP):
                row, partner = entry(self.tab, self.entries(t) + k)
                target[row] += dot(vectors[partner], tile(k), 1, 0)

        def near(t, carry):
            products(t, lambda k: self.kept[(self.place + t) * GROUP + k])
            return carry

        def step(t, carry):
            ahead = t + RING - 1

            @pl.when(self.stored(ahead))
            def _():
                self.read(ahead).start()

            have = self.stored(t)

            @pl.when(have)
            def _():
                self.read(t).wait()

            @pl.when(jnp.logical_not(have))
            def _():
                self.rebuild(t)

            products(t, lambda k: self.ring[self.slot(t), k])
            return carry

        lax.fori_loop(0, self.near, near, 0)
        lax.fori_loop(self.near, self.steps, step, 0)


def load_vectors(sz, tab, pieces, vbuf, sem):
    copies = []
    for s, piece in enumerate(pieces):
        if piece.shape[0] == sz.blocks and sz.cols > 1:
            target = vbuf
        else:
            owner = lax.rem(tab[sz.head] - s + sz.cols, sz.cols)
            target = vbuf.at[pl.ds(owner * sz.own, sz.own)]
        copies.append(pltpu.make_async_copy(piece, target, sem.at[s]))
    for copy in copies:
        copy.start()
    return copies


def sweep_cost(sz, entries):
    return pl.CostEstimate(
        flops=2 * entries * sz.width**2 * sz.vectors * 4,
        bytes_accessed=2 * entries * sz.width**2,
        transcendentals=0,
    )


def geometry_specs(sz):
    return [ANY_SPEC, VMEM_SPEC] + [ANY_SPEC] * (sz.peers - 1)


def split_geometry(sz, refs):
    return (refs[0], refs[1], refs[2 : sz.peers + 1]), refs[sz.peers + 1 :]


def slot_products(sz, table, tiles, geometry, pieces, inverse):
    count = len(pieces)
    others = sz.peers - 1
    with_picks = inverse is not None

    def kernel(tab, kept, store, *refs):
        blocks, refs = split_geometry(sz, refs)
        if with_picks:
            inverse_ref, refs = refs[0], refs[1:]
        piece_refs, refs = refs[:count], refs[count:]
        outs, refs = refs[:others], refs[others:]
        if with_picks:
            picks, refs = refs[:others], refs[others:]
        total, refs = refs[0], refs[1:]
        stream = Stream(sz, tab, "S", (kept, store), blocks, refs)
        vbuf = refs[0]
        copies = load_vectors(sz, tab, piece_refs, vbuf, refs[3])
        stream.begin()
        total[...] = jnp.zeros(total.shape, F32)
        for copy in copies:
            copy.wait()
        if with_picks:
            for m in range(1, sz.peers):
                for q in range(sz.cap):
                    b = jnp.minimum(tab[sz.mine + m * sz.cap + q], sz.blocks - 1)
                    picks[m - 1][q] = vbuf[b]
        stream.run(vbuf, total)
        for m in range(1, sz.peers):
            for q in range(sz.cap):
                products = total[m * sz.cap + q]
                if with_picks:
                    products = dot(inverse_ref[...], products, 1, 0, lax.Precision.HIGHEST)
                outs[m - 1][q] = products.astype(BF16)

    dims = (sz.cap, sz.vectors, sz.width)
    shapes = (jax.ShapeDtypeStruct(dims, BF16),) * others
    args = [table, *tiles, *geometry]
    specs = [SMEM_SPEC, VMEM_SPEC, HBM_SPEC] + geometry_specs(sz)
    if with_picks:
        shapes *= 2
        args.append(inverse)
        specs.append(VMEM_SPEC)
    return pl.pallas_call(
        kernel,
        out_shape=shapes,
        in_specs=specs + [ANY_SPEC] * count,
        out_specs=(VMEM_SPEC,) * len(shapes),
        scratch_shapes=[pltpu.VMEM((sz.slots + 1, sz.vectors, sz.width), F32)]
        + sweep_scratch(sz, sz.blocks),
        compiler_params=params(sz.limit),
        cost_estimate=sweep_cost(sz, 12),
    )(*args, *pieces)


def local_products(sz, table, tiles, geometry, pieces, names, earlier):
    count = len(pieces)
    first = earlier is None

    def kernel(tab, kept, store, *refs):
        blocks, refs = split_geometry(sz, refs)
        piece_refs, refs = refs[:count], refs[count:]
        if not first:
            summed, refs = refs[0], refs[1:]
        out, total, refs = refs[0], refs[1], refs[2:]
        stream = Stream(sz, tab, names, (kept, store), blocks, refs)
        vbuf = refs[0]
        copies = load_vectors(sz, tab, piece_refs, vbuf, refs[3])
        stream.begin()
        if first:
            total[...] = jnp.zeros(total.shape, F32)
        else:
            total[0 : sz.own] = summed[...]
        for copy in copies:
            copy.wait()
        stream.run(vbuf, total)
        out[...] = total[0 : sz.own]

    args = [table, *tiles, *geometry, *pieces]
    specs = [SMEM_SPEC, VMEM_SPEC, HBM_SPEC] + geometry_specs(sz) + [ANY_SPEC] * count
    if not first:
        args.append(earlier)
        specs.append(VMEM_SPEC)
    return pl.pallas_call(
        kernel,
        out_shape=jax.ShapeDtypeStruct((sz.own, sz.vectors, sz.width), F32),
        in_specs=specs,
        out_specs=VMEM_SPEC,
        scratch_shapes=[pltpu.VMEM((sz.own + 1, sz.vectors, sz.width), F32)]
        + sweep_scratch(sz, sz.blocks),
        compiler_params=params(sz.limit),
        cost_estimate=sweep_cost(sz, sum(dict(zip("01", (18, 44)))[name] for name in names)),
    )(*args)


def far_products(sz, table, tiles, geometry, summed, far, returned, root, inverse):
    cells_total = sz.blocks * sz.width * sz.peers
    last = inverse is not None
    many = len(far)

    def kernel(tab, kept, store, *refs):
        blocks, refs = split_geometry(sz, refs)
        summed_ref, root_ref, refs = refs[0], refs[1], refs[2:]
        if last:
            inverse_ref, refs = refs[0], refs[1:]
        far_refs, refs = refs[:many], refs[many:]
        back_refs, refs = refs[: sz.peers - 1], refs[sz.peers - 1 :]
        out, gram_out, total, refs = refs[0], refs[1], refs[2], refs[3:]
        stream = Stream(sz, tab, "2", (kept, store), blocks, refs[:7])
        vbuf, sem = refs[0], refs[3]
        if many == 1:
            copies = [pltpu.make_async_copy(far_refs[0], vbuf, sem.at[0])]
        else:
            copies = [
                pltpu.make_async_copy(far_refs[m - 1], vbuf.at[pl.ds(m * sz.cap, sz.cap)], sem.at[m])
                for m in range(1, sz.peers)
            ]
        for copy in copies:
            copy.start()
        stream.begin()
        z = tab[sz.head]
        total[0 : sz.own] = summed_ref[...]
        back = refs[-1] if last else total
        if last:
            back[...] = jnp.zeros(back.shape, F32)
        for m in range(1, sz.peers):
            for q in range(sz.cap):
                b = tab[sz.mine + m * sz.cap + q]

                @pl.when(divide(b, sz.own) == z)
                def _(m=m, q=q, b=b):
                    back[b - z * sz.own] += back_refs[m - 1][q].astype(F32)

        for copy in copies:
            copy.wait()
        stream.run(vbuf, total)
        gram = jnp.zeros((sz.vectors, sz.vectors), F32)
        for b in range(sz.own):
            root_row = root_ref[pl.ds(z * sz.own + b, 1), :]
            mapped = root_row * total[b]
            if last:
                mapped = dot(inverse_ref[...], mapped, 1, 0, lax.Precision.HIGHEST)
                mapped += root_row * back[b]
                out[b] = mapped
            else:
                out[b] = (root_row * mapped).astype(BF16)
            gram += dot(mapped, mapped, 1, 1, lax.Precision.HIGHEST)
        gram_out[...] = gram / cells_total

    args = [table, *tiles, *geometry, summed, root]
    specs = [SMEM_SPEC, VMEM_SPEC, HBM_SPEC] + geometry_specs(sz) + [VMEM_SPEC] * 2
    if last:
        args.append(inverse)
        specs.append(VMEM_SPEC)
    args += [*far, *returned]
    specs += [ANY_SPEC] * many + [VMEM_SPEC] * len(returned)
    return pl.pallas_call(
        kernel,
        out_shape=(
            jax.ShapeDtypeStruct((sz.own, sz.vectors, sz.width), F32 if last else BF16),
            jax.ShapeDtypeStruct((sz.vectors, sz.vectors), F32),
        ),
        in_specs=specs,
        out_specs=(VMEM_SPEC, VMEM_SPEC),
        scratch_shapes=[pltpu.VMEM((sz.own + 1, sz.vectors, sz.width), F32)]
        + sweep_scratch(sz, sz.slots)
        + [pltpu.VMEM((sz.own, sz.vectors, sz.width), F32)] * last,
        compiler_params=params(sz.limit),
        cost_estimate=sweep_cost(sz, 20),
    )(*args)


def inverse_factor(gram):
    n = gram.shape[0]
    eye = (
        lax.broadcasted_iota(jnp.int32, (n, n), 0) == lax.broadcasted_iota(jnp.int32, (n, n), 1)
    ).astype(F32)
    whole = jnp.concatenate([gram, eye], axis=1)
    chunk = 8
    parts = [whole[i : i + chunk] for i in range(0, n, chunk)]
    row_ids = lax.broadcasted_iota(jnp.int32, (chunk, 1), 0)
    for k in range(n):
        at, inside = k // chunk, k % chunk
        row = parts[at][inside : inside + 1]
        pivot = row[:, k : k + 1]
        ratio = row / pivot
        for j in range(at, n // chunk):
            factor = parts[j][:, k : k + 1]
            if j == at:
                if inside == chunk - 1:
                    continue
                factor = jnp.where(row_ids > inside, factor, 0.0)
            parts[j] = parts[j] - factor * ratio
    out = []
    for j in range(n // chunk):
        diagonal = jnp.sum(
            parts[j][:, :n] * eye[j * chunk : (j + 1) * chunk], axis=1, keepdims=True
        )
        out.append(parts[j][:, n:] * lax.rsqrt(diagonal))
    return jnp.concatenate(out, axis=0)


def factor_call(sz, gram):
    def kernel(gram_ref, out):
        out[...] = inverse_factor(gram_ref[...])

    return pl.pallas_call(
        kernel,
        out_shape=jax.ShapeDtypeStruct((sz.vectors, sz.vectors), F32),
        in_specs=[VMEM_SPEC],
        out_specs=VMEM_SPEC,
        compiler_params=params(sz.limit),
    )(gram)


def normalize(sz, table, gram, mapped):
    share = sz.vectors // sz.cols

    def kernel(tab, gram_ref, mapped_ref, *refs):
        outs, buf = refs[: sz.cols], refs[sz.cols]
        inverse = inverse_factor(gram_ref[...])
        z = tab[sz.head]
        for b in range(sz.own):
            buf[...] = dot(inverse, mapped_ref[b], 1, 0, lax.Precision.HIGHEST)
            for s in range(sz.cols):
                to = lax.rem(z + s, sz.cols)
                outs[s][b] = buf[pl.ds(pl.multiple_of(to * share, share), share)].astype(BF16)

    return pl.pallas_call(
        kernel,
        out_shape=(jax.ShapeDtypeStruct((sz.own, share, sz.width), BF16),) * sz.cols,
        in_specs=[SMEM_SPEC, VMEM_SPEC, VMEM_SPEC],
        out_specs=(VMEM_SPEC,) * sz.cols,
        scratch_shapes=[pltpu.VMEM((sz.vectors, sz.width), F32)],
        compiler_params=params(sz.limit),
    )(table, gram, mapped)


def assemble(sz, table, pieces):
    share = sz.vectors // sz.cols

    def kernel(tab, *refs):
        out = refs[-1]
        z = tab[sz.head]
        for s in range(sz.cols):
            owner = lax.rem(z - s + sz.cols, sz.cols)
            for b in range(sz.own):
                out[owner * sz.own + b] = refs[s][b].astype(F32)

    return pl.pallas_call(
        kernel,
        out_shape=jax.ShapeDtypeStruct((sz.blocks, share, sz.width), F32),
        in_specs=[SMEM_SPEC] + [VMEM_SPEC] * sz.cols,
        out_specs=VMEM_SPEC,
        compiler_params=params(sz.limit),
    )(table, *pieces)


def body(positions, scales, start_vectors, send_list, pair_rows, pair_partner):
    sz = Sizes(positions, start_vectors, send_list, pair_rows)
    where = jnp.stack([lax.axis_index("cells"), lax.axis_index("cols")]).astype(jnp.int32)
    n = sz.cols

    pairs = spread(
        jnp.concatenate([pair_rows.reshape(1, -1), pair_partner.reshape(1, -1)], axis=0), "cols"
    )
    lists = send_list.reshape(1, -1)
    send_all = jnp.concatenate([lists] + exchange([lists] * sz.peers, "cells"), axis=0)
    outgoing = outgoing_blocks(sz, lists, where, positions, scales, start_vectors)
    bundles = exchange((None,) + tuple(outgoing), "cells")

    table = build_table(sz, pairs, send_all, where)
    near_kept, *earlier = build_tiles(sz, table, "01", positions, scales, [], None)
    far_kept, store, sums = build_tiles(sz, table, "S2", positions, scales, bundles, earlier)
    near_tiles, far_tiles = (near_kept, store), (far_kept, store)
    geometry = (positions, scales, *bundles)

    partial = group_sums(sz, table, spread(sums, "cols"))
    partials = [partial] + exchange([partial] * sz.peers, "cells")
    near, far, root = scale_start(sz, table, send_all, where, partials, start_vectors, bundles)

    sent = slot_products(sz, table, far_tiles, geometry, [near], None)
    returned = exchange((None,) + tuple(sent), "cells")
    summed = local_products(sz, table, near_tiles, geometry, [near], "01", None)
    scaled, gram = far_products(
        sz, table, far_tiles, geometry, summed, [far], returned, root, None
    )

    pieces = spread(scaled, "cols")
    gram = butterfly(sum(spread(gram, "cols")), "cells")
    summed = local_products(sz, table, near_tiles, geometry, [scaled], "0", None)
    first_inverse = factor_call(sz, gram)
    pieces, summed, first_inverse = lax.optimization_barrier((pieces, summed, first_inverse))
    sent = slot_products(sz, table, far_tiles, geometry, pieces, first_inverse)
    sent, picks = sent[: sz.peers - 1], sent[sz.peers - 1 :]
    far_pieces = exchange((None,) + tuple(picks), "cells")
    returned = exchange((None,) + tuple(sent), "cells")
    summed = local_products(sz, table, near_tiles, geometry, pieces, "1", summed)
    mapped, gram = far_products(
        sz, table, far_tiles, geometry, summed, far_pieces, returned, root, first_inverse
    )
    gram = butterfly(butterfly(gram, "cells"), "cols")
    shares = normalize(sz, table, gram, mapped)
    arrived = [shares[0]] + [
        lax.ppermute(shares[s], "cols", [(i, (i + s) % n) for i in range(n)]) for s in range(1, n)
    ]
    return assemble(sz, table, arrived)


def solution(mesh):
    in_specs = (
        P(("lineage", "cells"), None, None),
        P(("lineage", "cells"), None),
        P(("lineage", "cells"), None, None),
        P(("lineage", "cells"), None, None),
        P(("lineage", "cells"), "cols", None),
        P(("lineage", "cells"), "cols", None),
    )
    out_specs = P(("lineage", "cells"), "cols", None)
    return jax.shard_map(body, mesh=mesh, in_specs=in_specs, out_specs=out_specs, check_vma=False)
```
